512 devices in a mesh: angle: 16 (over y, core), tile: 32 (over x, z).
Axes of the slice: x: 4, y: 8, z: 8, core: 2. Of those that a mesh axis runs over, the one named last changes fastest.
Arguments:
- patches: bfloat16 [16, 256, 2, 128, 128], P('angle', 'tile'), may hold values from -6 to 6
- magnitudes: bfloat16 [16, 2048, 128, 128], P('angle', 'tile'), may hold values from 0.099609375 to 3
- probe: float32 [2, 128, 128], replicated, may hold values from -6 to 6
- owners: int32 [16, 256, 1], P('angle', 'tile'), may hold values from 0 to 31; in each aligned block of 8 rows (0 to 7, 8 to 15, ..., all dimensions but the last counted through in order) at most 2 rows name the same one
- scan_rows: int32 [16, 256], P('angle', 'tile'), may hold values from 0 to 384
- scan_cols: int32 [16, 256], P('angle', 'tile'), may hold values from 0 to 896
- slab_rows: int32 [32, 16], P('tile'), may hold values from 0 to 2, as said below
- angle_tan: float32 [16], replicated, may hold values from -0.4 to 0.4
- prior_in: bfloat16 [16, 1, 3, 3], replicated, may hold values from -2 to 2
- prior_out: bfloat16 [1, 16, 3, 3], replicated, may hold values from -0.5 to 0.5
Outputs:
- volume: float32 [32, 32, 16, 1024], P('tile', 'angle')
The draws below stay inside these ranges and needn't reach their ends.
Inputs may be any that keep to these rules, and one draw needn't show every extreme that they name: `owners`: in the patches of one device, no owner is named by more than 2, and in some devices one owner is named exactly 2 times. Each row of slab_rows sums to 16, and in every row some slab has exactly 2 rows.
All inputs are finite; a program needn't handle non-finite values.
Results may differ from the reference program's by a relative error of at most 0.022.
Values may be sent and summed in bfloat16 or wider, within the bound.
A program may use at most 64 MiB of HBM per device.

```python
import math
import jax
import jax.numpy as jnp
import numpy as np
from jax import lax

P_SIZE = 128
H = 512
W = 1024
CH = 16
PATCH_DEV = 8
XW = 16
ANGLES = 16
TILES = 32
CAP = 2
SLAB_MEAN = 1
ROWCAP = 2


def draw_slab_rows(key, part):
    half = ANGLES // 2
    first, second = jax.random.split(jax.random.fold_in(key, 17))
    delta = jax.random.randint(first, (TILES, half), -SLAB_MEAN, SLAB_MEAN + 1)
    picked = jax.random.randint(second, (TILES,), 0, half)
    delta = jnp.where(jnp.arange(half)[None, :] == picked[:, None], SLAB_MEAN, delta)
    counts = jnp.stack([SLAB_MEAN + delta, SLAB_MEAN - delta], axis=-1)
    return counts.reshape(TILES, ANGLES).astype(jnp.int32)


def set_ends(values, key, least, top_value):
    index_at = [jax.random.randint(jax.random.fold_in(key, axis), (), 0, length) for axis, length in enumerate(values.shape)]
    longest = values.shape.index(max(values.shape))
    beside = index_at[:longest] + [(index_at[longest] + 1) % values.shape[longest]] + index_at[longest + 1:]
    return values.at[tuple(index_at)].set(least).at[tuple(beside)].set(top_value)


def levels(rng, dims, cuts, low, top_value):
    gain = 1.0
    for dim, shards_of in cuts:
        heights = jax.random.uniform(jax.random.fold_in(jax.random.fold_in(rng, 6), dim), (shards_of,), jnp.float32, low / len(cuts), top_value / len(cuts))
        gain = gain * jnp.repeat(jnp.exp(heights), dims[dim] // shards_of).reshape((-1,) + (1,) * (len(dims) - 1 - dim))
    return gain


def assign_block(rng, own, number, rows, amount, top, most, skew):
    sequence = jax.random.permutation(rng, amount)
    packed, usual = portions_of(amount, rows * top, most, skew, True), portions_of(amount, rows * top, most, skew, False)
    places = jnp.arange(amount)

    def named(tallies, rotation):
        used = int((tallies > 0).sum())
        fixed = max(1, used // 4)
        moved = fixed + (places - fixed + rotation * (used - fixed)) % max(1, amount - fixed)
        return jnp.zeros((amount,), jnp.int32).at[sequence[jnp.where(places < fixed, places, moved)]].set(jnp.asarray(tallies, jnp.int32))

    tallies = jnp.where(number % 4 == 0, named(packed, number // 4), named(usual, number - number // 4 - 1))
    mixed = jax.random.permutation(jax.random.fold_in(own, 3), amount)
    giver, sink = mixed[0:amount // 2 * 2:2], mixed[1:amount // 2 * 2:2]
    slack = jnp.minimum(tallies[giver] - 1, most - tallies[sink]) // 2
    slack = jnp.where((giver == sequence[0]) | (sink == sequence[0]) | (tallies[sink] == 0), 0, jnp.maximum(slack, 0))
    moved = jax.random.randint(jax.random.fold_in(own, 4), (amount // 2,), 0, 1 << 20) % (slack + 1)
    tallies = tallies.at[giver].add(-moved).at[sink].add(moved)
    items = jnp.searchsorted(jnp.cumsum(tallies), jnp.arange(rows * top), side="right").astype(jnp.int32)
    grid = items.reshape(top, rows).T
    grid = grid[jax.random.permutation(jax.random.fold_in(own, 1), rows)]
    rotation = jax.random.randint(jax.random.fold_in(own, 2), (rows, 1), 0, top)
    return jnp.take_along_axis(grid, (jnp.arange(top)[None, :] + rotation) % top, axis=1)


def portions_of(number_of, total, limit, slope, full):
    loads = [(1 << 20) // math.isqrt(standing ** slope) + 1 for standing in range(1, number_of + 1)]
    largest = limit if full else min(limit, max(-(-total // number_of), total * loads[0] // sum(loads)))
    least = 1 if total - largest >= number_of - 1 else 0
    given, rest = [largest] + [least] * (number_of - 1), total - largest - least * (number_of - 1)
    while rest > 0:
        movable = [i for i in range(1, number_of) if given[i] < largest] or [i for i in range(1, number_of) if given[i] < limit]
        mass, budget = sum([loads[i] for i in movable]), rest
        for i in movable:
            addition = min(limit - given[i], max(1, budget * loads[i] // mass), rest)
            given[i] = given[i] + addition
            rest = rest - addition
    return np.array(given)


def gaussian(key, shape, spread, limit, cuts=(), held_as=jnp.bfloat16):
    gain = levels(key, shape, cuts, -0.22, 0.18) if cuts else 1.0
    array = jax.random.normal(key, shape, jnp.float32) * spread * gain
    return jnp.minimum(jnp.maximum(array, -limit), limit).astype(held_as)


def setup_inputs(seed: int = 0) -> dict:
    seeds = jax.random.split(jax.random.key(seed), 11)
    patches = gaussian(seeds[0], (ANGLES, TILES * PATCH_DEV, 2, P_SIZE, P_SIZE), 1.0, 6.0, ((0, 16), (1, 32)))
    magnitudes = jnp.clip(jnp.exp(math.log(3.0) - 3.4051113 * jax.random.uniform(seeds[1], (ANGLES, TILES * TILES * CAP, P_SIZE, P_SIZE), jnp.float32) ** levels(seeds[1], (ANGLES, TILES * TILES * CAP, P_SIZE, P_SIZE), ((0, 16), (1, 32)), -0.2, 0.2)), 0.099609375, 3.0).astype(jnp.bfloat16)
    probe = gaussian(seeds[2], (2, P_SIZE, P_SIZE), 1.0, 6.0, (), jnp.float32)
    owners_keys = jax.random.split(jax.random.fold_in(seeds[3], 1), ANGLES * (TILES * PATCH_DEV) // PATCH_DEV)
    owners_turns = jax.random.permutation(jax.random.fold_in(seeds[3], 3), ANGLES * (TILES * PATCH_DEV) // PATCH_DEV)
    owners = jax.vmap(lambda own, number: assign_block(jax.random.fold_in(seeds[3], 2), own, number, PATCH_DEV, TILES, 1, CAP, 1))(owners_keys, owners_turns).reshape((ANGLES, TILES * PATCH_DEV, 1))
    scan_rows = set_ends(jax.random.randint(seeds[4], (ANGLES, TILES * PATCH_DEV), 0, H - P_SIZE + 1), jax.random.fold_in(seeds[4], 1), 0, H - P_SIZE).astype(jnp.int32)
    scan_cols = set_ends(jax.random.randint(seeds[5], (ANGLES, TILES * PATCH_DEV), 0, W - P_SIZE + 1), jax.random.fold_in(seeds[5], 1), 0, W - P_SIZE).astype(jnp.int32)
    slab_rows = draw_slab_rows(jax.random.fold_in(seeds[10], 71), 0)
    angle_tan = jnp.clip(jax.random.uniform(seeds[7], (ANGLES,), jnp.float32, -0.4, 0.4), -0.4, 0.4)
    prior_in = gaussian(seeds[8], (CH, 1, 3, 3), 9 ** -0.5, 2.0)
    prior_out = gaussian(seeds[9], (1, CH, 3, 3), (9 * CH) ** -0.5, 0.5)
    return dict(patches=patches, magnitudes=magnitudes, probe=probe, owners=owners, scan_rows=scan_rows, scan_cols=scan_cols, slab_rows=slab_rows, angle_tan=angle_tan, prior_in=prior_in, prior_out=prior_out)


def dft_table(side):
    index = jnp.arange(side, dtype=jnp.int32)
    product = index[:, None] * index[None, :] % side
    phase = product.astype(jnp.float32) * (2.0 * math.pi / side)
    scale = 1.0 / math.sqrt(side)
    real = jnp.cos(phase) * scale
    imag = -jnp.sin(phase) * scale
    upper = jnp.concatenate([real, imag], axis=1)
    lower = jnp.concatenate([-imag, real], axis=1)
    return jnp.concatenate([upper, lower], axis=0).astype(jnp.bfloat16)

def correct_one(wave, measured, table):
    side = wave.shape[1]
    left = table.T
    joined = jnp.concatenate([wave[0], wave[1]], axis=1)
    half = jnp.dot(joined, table, preferred_element_type=jnp.float32).astype(jnp.bfloat16)
    stacked = jnp.concatenate([half[:, :side], half[:, side:]], axis=0)
    spectrum = jnp.dot(left, stacked, preferred_element_type=jnp.float32)
    real_part = spectrum[:side]
    imag_part = spectrum[side:]
    factor = measured.astype(jnp.float32) / jnp.sqrt(real_part * real_part + imag_part * imag_part + 0.25)
    target = jnp.concatenate([real_part * factor, imag_part * factor], axis=1).astype(jnp.bfloat16)
    back = jnp.dot(target, left, preferred_element_type=jnp.float32).astype(jnp.bfloat16)
    stacked_back = jnp.concatenate([back[:, :side], back[:, side:]], axis=0)
    result = jnp.dot(table, stacked_back, preferred_element_type=jnp.float32)
    return jnp.stack([result[:side], result[side:]], axis=0).astype(jnp.bfloat16)

def backproject(sino, angle_tan):
    count = sino.shape[1]
    offsets = jnp.arange(XW, dtype=jnp.float32) - (XW - 1) / 2.0
    columns = jnp.arange(W, dtype=jnp.float32)

    def add_angle(total, item):
        rows, tangent = item
        where = columns[None, :] + offsets[:, None] * tangent
        lower = jnp.floor(where)
        frac = where - lower
        low_index = lower.astype(jnp.int32)
        high_index = low_index + 1
        low_ok = ((low_index >= 0) & (low_index < W)).astype(jnp.float32)
        high_ok = ((high_index >= 0) & (high_index < W)).astype(jnp.float32)
        low_val = jnp.take(rows, jnp.clip(low_index, 0, W - 1), axis=1) * low_ok
        high_val = jnp.take(rows, jnp.clip(high_index, 0, W - 1), axis=1) * high_ok
        return (total + (1.0 - frac) * low_val + frac * high_val, None)
    start = jnp.zeros((count, XW, W), jnp.float32)
    total, unused = lax.scan(add_angle, start, (sino, angle_tan))
    return total / sino.shape[0]

def prior(slices, prior_in, prior_out):
    numbers = ('NCHW', 'OIHW', 'NCHW')
    rounded = slices.astype(jnp.bfloat16)[:, None].astype(jnp.float32)
    hidden = lax.conv_general_dilated(rounded, prior_in.astype(jnp.float32), (1, 1), 'SAME', dimension_numbers=numbers)
    hidden = jnp.maximum(hidden, 0.0).astype(jnp.bfloat16).astype(jnp.float32)
    extra = lax.conv_general_dilated(hidden, prior_out.astype(jnp.float32), (1, 1), 'SAME', dimension_numbers=numbers)
    return slices + extra[:, 0]

def reference(patches, magnitudes, probe, owners, scan_rows, scan_cols, slab_rows, angle_tan, prior_in, prior_out):
    table = dft_table(P_SIZE)
    sources = jnp.arange(TILES, dtype=jnp.int32)

    def one_angle(item):
        waves, stored, owner_all, rows_all, cols_all = item
        owner = owner_all[:, 0].reshape(TILES, PATCH_DEV)
        member = (owner[:, :, None] == sources[None, None, :]).astype(jnp.int32)
        rank = lax.optimization_barrier(jnp.sum((jnp.cumsum(member, axis=1) - member) * member, axis=2))
        index = (owner * (TILES * CAP) + sources[:, None] * CAP + rank).reshape(-1)
        measured = stored[index]
        fixed = lax.map(lambda pair: correct_one(pair[0], pair[1], table), (waves, measured))
        fixed = fixed.astype(jnp.float32)
        contrib = (probe[0] * fixed[:, 1] - probe[1] * fixed[:, 0]) * 0.25

        def place(step, canvas):
            row = rows_all[step]
            col = cols_all[step]
            piece = lax.dynamic_slice(canvas, (row, col), (P_SIZE, P_SIZE)) + contrib[step]
            return lax.dynamic_update_slice(canvas, piece, (row, col))
        return lax.fori_loop(0, waves.shape[0], place, jnp.zeros((H, W), jnp.float32))
    projection = lax.map(one_angle, (patches, magnitudes, owners, scan_rows, scan_cols))
    strip_rows = H // TILES
    strips = projection.reshape(ANGLES, TILES, strip_rows, W)
    starts = jnp.cumsum(slab_rows, axis=1) - slab_rows
    within = jnp.arange(ROWCAP, dtype=jnp.int32)

    def one_strip(item):
        strip, start, count = item
        index = jnp.clip(start[:, None] + within[None, :], 0, strip_rows - 1)
        valid = (within[None, :] < count[:, None]).astype(jnp.float32)
        picked = strip[:, index] * valid[None, :, :, None]

        def one_slab(slab):
            return prior(backproject(slab, angle_tan), prior_in, prior_out)
        slabs = lax.map(one_slab, jnp.moveaxis(picked, 1, 0))
        return slabs.reshape(ANGLES * ROWCAP, XW, W)
    return lax.map(one_strip, (jnp.moveaxis(strips, 1, 0), starts, slab_rows))
```

```python
import functools
import math

import jax
import jax.numpy as jnp
import numpy as np
from jax import lax
from jax.experimental import pallas as pl
from jax.experimental.pallas import tpu as pltpu
from jax.sharding import PartitionSpec as P

H = 512
W = 1024
XW = 16
CH = 16
SIDE = 128
COUNT = 8
TX = 4
TZ = 8
TILES = TX * TZ
ANGLES = 16
STRIP = H // TILES
SPREAD = 4
SHIFTS = 2 * SPREAD + 1
MESH = pl.DeviceIdType.MESH
BF = jnp.bfloat16
F32 = jnp.float32


def dft_table(side):
    index = np.arange(side)
    phase = ((index[:, None] * index[None, :]) % side).astype(np.float32)
    phase = phase * np.float32(2.0 * math.pi / side)
    scale = np.float32(1.0 / math.sqrt(side))
    real = np.cos(phase) * scale
    imag = -np.sin(phase) * scale
    upper = np.concatenate([real, imag], axis=1)
    lower = np.concatenate([-imag, real], axis=1)
    return np.concatenate([upper, lower], axis=0).astype(np.float32)


def exchange_kernel(owners, mags, out, recv, send_sem, recv_sem, own_sem):
    a = lax.axis_index("angle")
    me = lax.axis_index("tile")
    barrier = pltpu.get_barrier_semaphore()

    def greet(i, c):
        peer = lax.rem(me + i, TILES)
        pl.semaphore_signal(barrier, inc=1, device_id=(a, peer), device_id_type=MESH)
        return c

    lax.fori_loop(1, TILES, greet, 0)
    pl.semaphore_wait(barrier, TILES - 1)

    own = pltpu.make_async_copy(mags.at[pl.ds(me * 2, 2)], recv.at[pl.ds(me * 2, 2)], own_sem)
    own.start()

    def remote(i):
        peer = lax.rem(me + i, TILES)
        return pltpu.make_async_remote_copy(
            src_ref=mags.at[pl.ds(peer * 2, 2)],
            dst_ref=recv.at[pl.ds(me * 2, 2)],
            send_sem=send_sem.at[i],
            recv_sem=recv_sem.at[i],
            device_id=(a, peer),
            device_id_type=MESH,
        )

    def start(i, c):
        remote(i).start()
        return c

    lax.fori_loop(1, TILES, start, 0)

    def finish(i, c):
        source = lax.rem(me - i + TILES, TILES)
        copy = pltpu.make_async_remote_copy(
            src_ref=mags.at[pl.ds(source * 2, 2)],
            dst_ref=recv.at[pl.ds(source * 2, 2)],
            send_sem=send_sem.at[i],
            recv_sem=recv_sem.at[i],
            device_id=(a, source),
            device_id_type=MESH,
        )
        copy.wait_recv()
        copy.wait_send()
        return c

    lax.fori_loop(1, TILES, finish, 0)
    own.wait()

    ids = [owners[0, k] for k in range(COUNT)]
    for k in range(COUNT):
        rank = jnp.int32(0)
        for j in range(k):
            rank = rank + jnp.where(ids[j] == ids[k], 1, 0).astype(jnp.int32)
        out[k] = recv[ids[k] * 2 + rank]


def canvas_kernel(rows, cols, patches, level, probe, table, table_t, out, canvas):
    canvas[...] = jnp.zeros_like(canvas)
    pair = 2
    for g in range(COUNT // pair):
        ks = [g * pair + j for j in range(pair)]
        joined = jnp.concatenate(
            [jnp.concatenate([patches[k, 0], patches[k, 1]], axis=1) for k in ks], axis=0
        )
        half = jnp.dot(joined, table[...], preferred_element_type=F32).astype(BF)
        stacked = jnp.concatenate(
            [
                jnp.concatenate([half[j * SIDE : (j + 1) * SIDE, q * SIDE : (q + 1) * SIDE] for j in range(pair)], axis=1)
                for q in range(2)
            ],
            axis=0,
        )
        spectrum = jnp.dot(table_t[...], stacked, preferred_element_type=F32)
        real = spectrum[:SIDE]
        imag = spectrum[SIDE:]
        measured = jnp.concatenate([level[k] for k in ks], axis=1).astype(F32)
        factor = measured * lax.rsqrt(real * real + imag * imag + 0.25)
        real = (real * factor).astype(BF)
        imag = (imag * factor).astype(BF)
        target = jnp.concatenate(
            [
                jnp.concatenate([real[:, j * SIDE : (j + 1) * SIDE], imag[:, j * SIDE : (j + 1) * SIDE]], axis=1)
                for j in range(pair)
            ],
            axis=0,
        )
        back = jnp.dot(target, table_t[...], preferred_element_type=F32).astype(BF)
        stacked = jnp.concatenate(
            [
                jnp.concatenate([back[j * SIDE : (j + 1) * SIDE, q * SIDE : (q + 1) * SIDE] for j in range(pair)], axis=1)
                for q in range(2)
            ],
            axis=0,
        )
        result = jnp.dot(table[...], stacked, preferred_element_type=F32)
        for j in range(pair):
            k = ks[j]
            part = slice(j * SIDE, (j + 1) * SIDE)
            contrib = (probe[0] * result[SIDE:, part] - probe[1] * result[:SIDE, part]) * 0.25
            row = rows[0, k]
            col = cols[0, k]
            low_row = row // 8
            low_col = col // SIDE
            wide = jnp.concatenate([contrib, jnp.zeros((SIDE, SIDE), F32)], axis=1)
            wide = pltpu.roll(wide, col - low_col * SIDE, 1)
            tall = jnp.concatenate([wide, jnp.zeros((8, 2 * SIDE), F32)], axis=0)
            tall = pltpu.roll(tall, row - low_row * 8, 0)
            at = (pl.ds(pl.multiple_of(low_row * 8, 8), SIDE + 8), pl.ds(pl.multiple_of(low_col * SIDE, SIDE), 2 * SIDE))
            canvas[at] = canvas[at] + tall
    out[...] = canvas[:H, :W].astype(BF)


def strip_kernel(
    lengths, canvas, out, mine, from_x, part, from_z, sel, pieces, sino, own_sem, xs, xr, zs, zr, as_, ar
):
    a = lax.axis_index("angle")
    me = lax.axis_index("tile")
    x = me // TZ
    z = lax.rem(me, TZ)
    barrier = pltpu.get_barrier_semaphore()
    rows = TZ * STRIP

    def at_x(i):
        return lax.rem(x + i, TX) * TZ + z

    def at_z(i):
        return x * TZ + lax.rem(z + i, TZ)

    def greet(which, axis_angle):
        def run(i, c):
            if axis_angle:
                target = (lax.rem(a + i, ANGLES), me)
            else:
                target = (a, which(i))
            pl.semaphore_signal(barrier, inc=1, device_id=target, device_id_type=MESH)
            return c

        return run

    lax.fori_loop(1, TX, greet(at_x, False), 0)
    lax.fori_loop(1, TZ, greet(at_z, False), 0)
    lax.fori_loop(1, ANGLES, greet(None, True), 0)
    pl.semaphore_wait(barrier, TX + TZ + ANGLES - 3)

    own = pltpu.make_async_copy(canvas.at[pl.ds(x * rows, rows)], mine, own_sem)
    own.start()

    def copy_x(i):
        peer = at_x(i)
        return pltpu.make_async_remote_copy(
            src_ref=canvas.at[pl.ds((peer // TZ) * rows, rows)],
            dst_ref=from_x.at[i],
            send_sem=xs.at[i],
            recv_sem=xr.at[i],
            device_id=(a, peer),
            device_id_type=MESH,
        )

    for i in (2, 1, 3):
        copy_x(i).start()

    row_id = lax.broadcasted_iota(jnp.int32, (16, 128), 0)
    lane_id = lax.broadcasted_iota(jnp.int32, (16, 128), 1)
    within = row_id % 2
    same = (row_id // 2) == (lane_id // 16)
    place = lane_id % 16 - within
    begin = jnp.int32(0)
    for b in range(ANGLES):
        length = lengths[0, b]
        hit = same & (place == begin) & (within < length)
        sel[b] = hit.astype(F32).astype(BF)
        begin = begin + length

    own.wait()
    for i in (1, 3, 2):
        copy_x(i).wait_recv()
    total = mine[...].astype(F32)
    for i in range(1, TX):
        total = total + from_x[i].astype(F32)
    total = total.astype(BF)
    for j in range(TZ):
        part[j] = total[j * STRIP : (j + 1) * STRIP]

    def copy_z(i):
        peer = at_z(i)
        return pltpu.make_async_remote_copy(
            src_ref=part.at[lax.rem(peer, TZ)],
            dst_ref=from_z.at[i],
            send_sem=zs.at[i],
            recv_sem=zr.at[i],
            device_id=(a, peer),
            device_id_type=MESH,
        )

    for i in (4, 3, 5, 2, 6, 1, 7):
        copy_z(i).start()
    strip = part[z].astype(F32)
    for i in (1, 7, 2, 6, 3, 5, 4):
        copy_z(i).wait_recv()
        strip = strip + from_z[i].astype(F32)
    strip = strip.astype(BF)
    blocks = jnp.concatenate([strip[:, c * 128 : (c + 1) * 128] for c in range(W // 128)], axis=0)
    chosen = jnp.dot(sel[...].reshape(ANGLES * 16, 128), blocks, preferred_element_type=F32)
    pieces[...] = chosen.astype(BF).reshape(ANGLES, 16, 128)

    def copy_a(i):
        peer = lax.rem(a + i, ANGLES)
        return pltpu.make_async_remote_copy(
            src_ref=pieces.at[peer],
            dst_ref=sino.at[a],
            send_sem=as_.at[i],
            recv_sem=ar.at[i],
            device_id=(peer, me),
            device_id_type=MESH,
        )

    def start_a(i, c):
        copy_a(i).start()
        return c

    lax.fori_loop(1, ANGLES, start_a, 0)
    sino[a] = pieces[a]

    def finish_a(i, c):
        source = lax.rem(a - i + ANGLES, ANGLES)
        pltpu.make_async_remote_copy(
            src_ref=pieces.at[source],
            dst_ref=sino.at[source],
            send_sem=as_.at[i],
            recv_sem=ar.at[i],
            device_id=(source, me),
            device_id_type=MESH,
        ).wait_recv()
        return c

    lax.fori_loop(1, ANGLES, finish_a, 0)
    out[...] = sino[...]
    for i in range(1, TX):
        copy_x(i).wait_send()
    for i in range(1, TZ):
        copy_z(i).wait_send()

    def sent_a(i, c):
        copy_a(i).wait_send()
        return c

    lax.fori_loop(1, ANGLES, sent_a, 0)


def shifted(values, step):
    if step == 0:
        return values
    lane = lax.broadcasted_iota(jnp.int32, values.shape, 1) + step
    rolled = pltpu.roll(values, (-step) % W, 1)
    return jnp.where((lane >= 0) & (lane < W), rolled, 0.0)


def slab_kernel(first, second, tangents, sino, out, flat, k_in, k_out):
    rows = SHIFTS * XW
    row = lax.broadcasted_iota(jnp.int32, (rows, ANGLES), 0)
    offset = (row % XW).astype(F32) - (XW - 1) / 2.0
    shift = (row // XW).astype(F32) - float(SPREAD)
    weight = jnp.maximum(1.0 - jnp.abs(offset * tangents[...] - shift), 0.0) * (1.0 / ANGLES)
    high = weight.astype(BF)
    low = (weight - high.astype(F32)).astype(BF)
    weights = jnp.concatenate([high, low], axis=1)

    r16 = lax.broadcasted_iota(jnp.int32, (XW, 128), 0)
    lane = lax.broadcasted_iota(jnp.int32, (XW, 128), 1)
    masks = [
        [((lane // XW == dj) & (lane % XW == r16 + di - 1)).astype(F32) for dj in range(3)] for di in range(3)
    ]
    for ch in range(CH):
        total = jnp.zeros((XW, 128), F32)
        for di in range(3):
            for dj in range(3):
                total = total + masks[di][dj] * first[ch, di * 3 + dj]
        k_in[ch * XW : (ch + 1) * XW, :] = total.astype(BF)
    near = [(lane % XW == r16 + di - 1) for di in range(3)]
    marks = [[(near[di] & (lane // XW == q)).astype(F32) for di in range(3)] for q in range(8)]
    for block in range(CH // 8):
        for dj in range(3):
            total = jnp.zeros((XW, 128), F32)
            for q in range(8):
                for di in range(3):
                    total = total + marks[q][di] * second[block * 8 + q, di * 3 + dj]
            k_out[dj * XW : (dj + 1) * XW, block * 128 : (block + 1) * 128] = total.astype(BF)

    flat[...] = sino[...].astype(F32).reshape(ANGLES * 16, 128)
    for r in range(2):
        rows_r = jnp.concatenate(
            [flat[pl.ds(2 * c + r, ANGLES, stride=16), :] for c in range(W // 128)], axis=1
        ).astype(BF)
        both = jnp.concatenate([rows_r, rows_r], axis=0)
        spread = jnp.dot(weights, both, preferred_element_type=F32)
        picture = jnp.zeros((XW, W), F32)
        for s in range(SHIFTS):
            picture = picture + shifted(spread[s * XW : (s + 1) * XW], s - SPREAD)
        rounded = picture.astype(BF).astype(F32)
        stack = jnp.concatenate([shifted(rounded, dj - 1) for dj in range(3)], axis=0).astype(BF)
        hidden = jnp.dot(k_in[:, : 3 * XW], stack, preferred_element_type=F32)
        hidden = jnp.maximum(hidden, 0.0).astype(BF)
        extra = jnp.dot(k_out[...], hidden, preferred_element_type=F32)
        for dj in range(3):
            picture = picture + shifted(extra[dj * XW : (dj + 1) * XW], dj - 1)
        out[r] = picture


def body(patches, magnitudes, probe, owners, scan_rows, scan_cols, slab_rows, angle_tan, prior_in, prior_out):
    vmem = pl.BlockSpec(memory_space=pltpu.VMEM)
    smem = pl.BlockSpec(memory_space=pltpu.SMEM)
    hbm = pl.BlockSpec(memory_space=pl.ANY)
    dma = pltpu.SemaphoreType.DMA
    limit = 48 * 1024 * 1024
    numbers = dft_table(SIDE)
    table = jnp.asarray(numbers).astype(BF)
    table_t = jnp.asarray(np.ascontiguousarray(numbers.T)).astype(BF)

    level = pl.pallas_call(
        exchange_kernel,
        out_shape=jax.ShapeDtypeStruct((COUNT, SIDE, SIDE), BF),
        in_specs=[smem, hbm],
        out_specs=vmem,
        scratch_shapes=[
            pltpu.VMEM((2 * TILES, SIDE, SIDE), BF),
            dma((TILES,)),
            dma((TILES,)),
            dma,
        ],
        compiler_params=pltpu.CompilerParams(collective_id=0, has_side_effects=True, vmem_limit_bytes=limit),
        name="frames",
    )(owners.reshape(1, COUNT), magnitudes[0])

    canvas = pl.pallas_call(
        canvas_kernel,
        out_shape=jax.ShapeDtypeStruct((H, W), BF),
        in_specs=[smem, smem, vmem, vmem, vmem, vmem, vmem],
        out_specs=vmem,
        scratch_shapes=[pltpu.VMEM((H + 8, W + SIDE), F32)],
        compiler_params=pltpu.CompilerParams(vmem_limit_bytes=limit),
        name="canvas",
    )(scan_rows, scan_cols, patches[0], level, probe, table, table_t)

    rows = TZ * STRIP
    sino = pl.pallas_call(
        strip_kernel,
        out_shape=jax.ShapeDtypeStruct((ANGLES, 16, 128), BF),
        in_specs=[smem, hbm],
        out_specs=vmem,
        scratch_shapes=[
            pltpu.VMEM((rows, W), BF),
            pltpu.VMEM((TX, rows, W), BF),
            pltpu.VMEM((TZ, STRIP, W), BF),
            pltpu.VMEM((TZ, STRIP, W), BF),
            pltpu.VMEM((ANGLES, 16, 128), BF),
            pltpu.VMEM((ANGLES, 16, 128), BF),
            pltpu.VMEM((ANGLES, 16, 128), BF),
            dma,
            dma((TX,)),
            dma((TX,)),
            dma((TZ,)),
            dma((TZ,)),
            dma((ANGLES,)),
            dma((ANGLES,)),
        ],
        compiler_params=pltpu.CompilerParams(collective_id=1, has_side_effects=True, vmem_limit_bytes=limit),
        name="strips",
    )(slab_rows, canvas)

    volume = pl.pallas_call(
        slab_kernel,
        out_shape=jax.ShapeDtypeStruct((2, XW, W), F32),
        in_specs=[smem, smem, vmem, vmem],
        out_specs=vmem,
        scratch_shapes=[
            pltpu.VMEM((ANGLES * 16, 128), F32),
            pltpu.VMEM((CH * XW, 128), BF),
            pltpu.VMEM((3 * XW, CH * XW), BF),
        ],
        compiler_params=pltpu.CompilerParams(vmem_limit_bytes=limit),
        name="slabs",
    )(
        prior_in.astype(F32).reshape(CH, 9),
        prior_out.astype(F32).reshape(CH, 9),
        angle_tan.reshape(1, ANGLES),
        sino,
    )
    return volume[None]


def solution(mesh):
    placed = (
        P("angle", "tile", None, None, None),
        P("angle", "tile", None, None),
        P(),
        P("angle", "tile", None),
        P("angle", "tile"),
        P("angle", "tile"),
        P("tile", None),
        P(),
        P(),
        P(),
    )
    return jax.shard_map(
        body, mesh=mesh, in_specs=placed, out_specs=P("tile", "angle", None, None), check_vma=False
    )
```

```python
import math

import jax
import jax.numpy as jnp
import numpy as np
from jax import lax
from jax.experimental import pallas as pl
from jax.experimental.pallas import tpu as pltpu
from jax.sharding import PartitionSpec as P

H = 512
W = 1024
XW = 16
CH = 16
SIDE = 128
COUNT = 8
TX = 4
TZ = 8
TILES = TX * TZ
ANGLES = 16
STRIP = H // TILES
SPREAD = 4
SHIFTS = 2 * SPREAD + 1
HALF = COUNT // 2
CHUNKS = 4
WIDE = W // CHUNKS
AHEAD = 3
ORDER = (4, 3, -3, 2, -2, 1, -1, 0)
CHAINS = ((1, 4, 0), (-1, 3, 0), (1, 3, HALF), (-1, 4, HALF))
MESH = pl.DeviceIdType.MESH
BF = jnp.bfloat16
F32 = jnp.float32


def dft_table(side):
    index = np.arange(side)
    phase = ((index[:, None] * index[None, :]) % side).astype(np.float32)
    phase = phase * np.float32(2.0 * math.pi / side)
    scale = np.float32(1.0 / math.sqrt(side))
    real = np.cos(phase) * scale
    imag = -np.sin(phase) * scale
    upper = np.concatenate([real, imag], axis=1)
    lower = np.concatenate([-imag, real], axis=1)
    return np.concatenate([upper, lower], axis=0).astype(np.float32)


def fused_kernel(
    owners, rows, cols, lengths, patches, mags, probe, table, table_t, out,
    f0, f1, f2, f3, f4, f5, f6, f7, c0, c1, c2, c3,
    waves, light, fwd, fwd_t, ids_out, ids_in, ids_s, spec, hot, placed, stage, from_x, mine, part, from_z, sel,
    pieces, sino, loc, xs, xr, cs, cr, is_, ir, ls, sxs, sxr, szs, szr, as_, ar,
):
    frames = (f0, f1, f2, f3, f4, f5, f6, f7)
    chains = (c0, c1, c2, c3)
    a = lax.axis_index("angle")
    me = lax.axis_index("tile")
    x = me // TZ
    z = lax.rem(me, TZ)
    rows_x = TZ * STRIP

    def at_x(i):
        return lax.rem(x + i, TX) * TZ + z

    def at_z(i):
        return x * TZ + lax.rem(z + i + TZ, TZ)

    local = [
        pltpu.make_async_copy(patches, waves, loc.at[8]),
        pltpu.make_async_copy(table, fwd, loc.at[9]),
        pltpu.make_async_copy(table_t, fwd_t, loc.at[10]),
        pltpu.make_async_copy(probe, light, loc.at[11]),
    ]
    for copy in local:
        copy.start()

    def source_z(d):
        return lax.rem(z + d + TZ, TZ)

    def own_frames(q):
        return pltpu.make_async_copy(
            mags.at[pl.ds((x * TZ + source_z(ORDER[q])) * 2, 2)], frames[q].at[pl.ds(x * 2, 2)], loc.at[q]
        )

    for q in range(TZ):
        own_frames(q).start()

    barrier = pltpu.get_barrier_semaphore()
    for i in range(1, TX):
        pl.semaphore_signal(barrier, inc=1, device_id=(a, at_x(i)), device_id_type=MESH)
    for i in range(1, TZ):
        pl.semaphore_signal(barrier, inc=1, device_id=(a, at_z(i)), device_id_type=MESH)

    def greet(i, c):
        pl.semaphore_signal(barrier, inc=1, device_id=(lax.rem(a + i, ANGLES), me), device_id_type=MESH)
        return c

    lax.fori_loop(1, ANGLES, greet, 0)

    mine_ids = [owners[0, k] for k in range(COUNT)]
    lane = lax.broadcasted_iota(jnp.int32, (8, 128), 1)
    vector = jnp.zeros((8, 128), jnp.int32)
    for k in range(COUNT):
        vector = jnp.where(lane == k, mine_ids[k], vector)
    ids_out[...] = vector
    pl.semaphore_wait(barrier, TX + TZ + ANGLES - 3)

    def copy_ids(i):
        return pltpu.make_async_remote_copy(
            src_ref=ids_out, dst_ref=ids_in.at[i], send_sem=is_.at[i], recv_sem=ir.at[i],
            device_id=(a, at_z(i)), device_id_type=MESH,
        )

    for i in (4, 3, 5, 2, 6, 1, 7):
        copy_ids(i).start()

    def copy_x(q, i):
        peer = at_x(i)
        return pltpu.make_async_remote_copy(
            src_ref=mags.at[pl.ds(((peer // TZ) * TZ + source_z(ORDER[q])) * 2, 2)],
            dst_ref=frames[q].at[pl.ds(x * 2, 2)],
            send_sem=xs.at[q, i], recv_sem=xr.at[q, i],
            device_id=(a, peer), device_id_type=MESH,
        )

    def start_x(q):
        for i in (2, 1, 3):
            copy_x(q, i).start()

    for q in range(AHEAD):
        start_x(q)

    row_id = lax.broadcasted_iota(jnp.int32, (16, 128), 0)
    lane_id = lax.broadcasted_iota(jnp.int32, (16, 128), 1)
    within = row_id % 2
    same = (row_id // 2) == (lane_id // 16)
    place = lane_id % 16 - within
    begin = jnp.int32(0)
    for b in range(ANGLES):
        length = lengths[0, b]
        hit = same & (place == begin) & (within < length)
        sel[b] = hit.astype(F32).astype(BF)
        begin = begin + length
    gap = lax.broadcasted_iota(jnp.int32, (H, 128), 0) - lax.broadcasted_iota(jnp.int32, (H, 128), 1)
    for k in range(COUNT):
        hot[:, k * SIDE : (k + 1) * SIDE] = (gap == rows[0, k]).astype(F32).astype(BF)

    pair = 2

    def stack(values):
        return jnp.concatenate(
            [
                jnp.concatenate(
                    [values[j * SIDE : (j + 1) * SIDE, p * SIDE : (p + 1) * SIDE] for j in range(pair)], axis=1
                )
                for p in range(2)
            ],
            axis=0,
        )

    for copy in local:
        copy.wait()
    for g in range(COUNT // pair):
        joined = jnp.concatenate(
            [jnp.concatenate([waves[k, 0], waves[k, 1]], axis=1) for k in range(g * pair, (g + 1) * pair)], axis=0
        )
        half = jnp.dot(joined, fwd[...], preferred_element_type=F32).astype(BF)
        spec[:, g * pair * SIDE : (g + 1) * pair * SIDE] = jnp.dot(
            fwd_t[...], stack(half), preferred_element_type=F32
        )

    for i in (1, 7, 2, 6, 3, 5, 4):
        copy_ids(i).wait_recv()
    to_scalar = pltpu.make_async_copy(ids_in, ids_s, ls)
    to_scalar.start()
    to_scalar.wait()

    def chosen(q):
        d = ORDER[q]
        ids = mine_ids if d == 0 else [ids_s[(-d) % TZ, 0, k] for k in range(COUNT)]

        def one(k):
            rank = jnp.int32(0)
            for j in range(k):
                rank = rank + jnp.where(ids[j] == ids[k], 1, 0).astype(jnp.int32)
            return (ids[k] & 7) == z, frames[q][((ids[k] >> 3) & 3) * 2 + (rank & 1)]

        return one

    def copy_chain(c, level):
        step = CHAINS[c][0]
        return pltpu.make_async_remote_copy(
            src_ref=chains[c].at[level], dst_ref=chains[c].at[level - 1],
            send_sem=cs.at[c, level], recv_sem=cr.at[c, level - 1],
            device_id=(a, at_z(step)), device_id_type=MESH,
        )

    for q in range(TZ):
        if q + AHEAD < TZ:
            start_x(q + AHEAD)
        own_frames(q).wait()
        for i in (1, 3, 2):
            copy_x(q, i).wait_recv()
        pick = chosen(q)
        d = ORDER[q]
        if d == 0:
            for c in range(4):
                copy_chain(c, 1).wait_recv()
            break
        for c in range(4):
            step, first, base = CHAINS[c]
            level = 4 if d == 4 else step * d
            if level < 1 or level > first:
                continue
            if level < first:
                copy_chain(c, level + 1).wait_recv()
            for k in range(HALF):
                hit, frame = pick(base + k)
                before = chains[c][level, k] if level < first else jnp.zeros((SIDE, SIDE), BF)
                chains[c][level, k] = jnp.where(hit, frame, before)
            copy_chain(c, level).start()

    for g in range(COUNT // pair):
        ks = [g * pair + j for j in range(pair)]
        measured = []
        for k in ks:
            hit, frame = pick(k)
            two = (0, 1) if k < HALF else (2, 3)
            came = chains[two[0]][0, k % HALF] + chains[two[1]][0, k % HALF]
            measured.append(jnp.where(hit, frame, came).astype(F32))
        part_g = slice(g * pair * SIDE, (g + 1) * pair * SIDE)
        real = spec[:SIDE, part_g]
        imag = spec[SIDE:, part_g]
        factor = jnp.concatenate(measured, axis=1) * lax.rsqrt(real * real + imag * imag + 0.25)
        real = (real * factor).astype(BF)
        imag = (imag * factor).astype(BF)
        target = jnp.concatenate(
            [
                jnp.concatenate([real[:, j * SIDE : (j + 1) * SIDE], imag[:, j * SIDE : (j + 1) * SIDE]], axis=1)
                for j in range(pair)
            ],
            axis=0,
        )
        back = jnp.dot(target, fwd_t[...], preferred_element_type=F32).astype(BF)
        result = jnp.dot(fwd[...], stack(back), preferred_element_type=F32)
        for j in range(pair):
            k = ks[j]
            at = slice(j * SIDE, (j + 1) * SIDE)
            contrib = (light[0] * result[SIDE:, at] - light[1] * result[:SIDE, at]) * 0.25
            col = cols[0, k]
            low = col >> 7
            wide = jnp.concatenate([contrib, jnp.zeros((SIDE, SIDE), F32)], axis=1)
            wide = pltpu.roll(wide, col & 127, 1).astype(BF)
            left = wide[:, :SIDE]
            right = wide[:, SIDE:]
            none = jnp.zeros((SIDE, SIDE), BF)
            for b in range(W // SIDE):
                placed[k * SIDE : (k + 1) * SIDE, b * SIDE : (b + 1) * SIDE] = jnp.where(
                    low == b, left, jnp.where(low + 1 == b, right, none)
                )

    def copy_s(n, i):
        return pltpu.make_async_remote_copy(
            src_ref=stage.at[n, i], dst_ref=from_x.at[n, i], send_sem=sxs.at[n, i], recv_sem=sxr.at[n, i],
            device_id=(a, at_x(i)), device_id_type=MESH,
        )

    def canvas_of(n, i):
        at = pl.ds(pl.multiple_of(lax.rem(x + i, TX) * rows_x, rows_x), rows_x)
        return jnp.dot(hot[at, :], placed[:, n * WIDE : (n + 1) * WIDE], preferred_element_type=F32)

    for n in range(CHUNKS):
        for i in (2, 1, 3):
            stage[n, i] = canvas_of(n, i).astype(BF)
            copy_s(n, i).start()
        mine[n] = canvas_of(n, 0)

    def copy_z(n, i):
        return pltpu.make_async_remote_copy(
            src_ref=part.at[n, lax.rem(z + i, TZ)], dst_ref=from_z.at[n, i],
            send_sem=szs.at[n, i], recv_sem=szr.at[n, i],
            device_id=(a, at_z(i)), device_id_type=MESH,
        )

    for n in range(CHUNKS):
        total = mine[n]
        for i in (1, 3, 2):
            copy_s(n, i).wait_recv()
            total = total + from_x[n, i].astype(F32)
        total = total.astype(BF)
        for j in range(TZ):
            part[n, j] = total[j * STRIP : (j + 1) * STRIP]
        for i in (4, 3, 5, 2, 6, 1, 7):
            copy_z(n, i).start()

    blocks = []
    for n in range(CHUNKS):
        strip = part[n, z].astype(F32)
        for i in (1, 7, 2, 6, 3, 5, 4):
            copy_z(n, i).wait_recv()
            strip = strip + from_z[n, i].astype(F32)
        strip = strip.astype(BF)
        blocks += [strip[:, c * 128 : (c + 1) * 128] for c in range(WIDE // 128)]
    picked = jnp.dot(
        sel[...].reshape(ANGLES * 16, 128), jnp.concatenate(blocks, axis=0), preferred_element_type=F32
    )
    pieces[...] = picked.astype(BF).reshape(ANGLES, 16, 128)

    def copy_a(i):
        peer = lax.rem(a + i, ANGLES)
        return pltpu.make_async_remote_copy(
            src_ref=pieces.at[peer], dst_ref=sino.at[a], send_sem=as_.at[i], recv_sem=ar.at[i],
            device_id=(peer, me), device_id_type=MESH,
        )

    def start_a(i, c):
        copy_a(i).start()
        return c

    lax.fori_loop(1, ANGLES, start_a, 0)
    sino[a] = pieces[a]

    for i in range(1, TZ):
        copy_ids(i).wait_send()
    for q in range(TZ):
        for i in range(1, TX):
            copy_x(q, i).wait_send()
    for c in range(4):
        for level in range(1, CHAINS[c][1] + 1):
            copy_chain(c, level).wait_send()
    for n in range(CHUNKS):
        for i in range(1, TX):
            copy_s(n, i).wait_send()
        for i in range(1, TZ):
            copy_z(n, i).wait_send()

    def finish_a(i, c):
        source = lax.rem(a - i + ANGLES, ANGLES)
        pltpu.make_async_remote_copy(
            src_ref=pieces.at[source], dst_ref=sino.at[source], send_sem=as_.at[i], recv_sem=ar.at[i],
            device_id=(source, me), device_id_type=MESH,
        ).wait_recv()
        return c

    lax.fori_loop(1, ANGLES, finish_a, 0)
    out[...] = sino[...]

    def sent_a(i, c):
        copy_a(i).wait_send()
        return c

    lax.fori_loop(1, ANGLES, sent_a, 0)


def shifted(values, step):
    if step == 0:
        return values
    lane = lax.broadcasted_iota(jnp.int32, values.shape, 1) + step
    rolled = pltpu.roll(values, (-step) % W, 1)
    return jnp.where((lane >= 0) & (lane < W), rolled, 0.0)


def slab_kernel(first, second, tangents, sino, out, flat, k_in, k_out):
    rows = SHIFTS * XW
    row = lax.broadcasted_iota(jnp.int32, (rows, ANGLES), 0)
    offset = (row % XW).astype(F32) - (XW - 1) / 2.0
    shift = (row // XW).astype(F32) - float(SPREAD)
    weight = jnp.maximum(1.0 - jnp.abs(offset * tangents[...] - shift), 0.0) * (1.0 / ANGLES)
    high = weight.astype(BF)
    low = (weight - high.astype(F32)).astype(BF)
    weights = jnp.concatenate([high, low], axis=1)

    r16 = lax.broadcasted_iota(jnp.int32, (XW, 128), 0)
    lane = lax.broadcasted_iota(jnp.int32, (XW, 128), 1)
    masks = [
        [((lane // XW == dj) & (lane % XW == r16 + di - 1)).astype(F32) for dj in range(3)] for di in range(3)
    ]
    for ch in range(CH):
        total = jnp.zeros((XW, 128), F32)
        for di in range(3):
            for dj in range(3):
                total = total + masks[di][dj] * first[ch, di * 3 + dj]
        k_in[ch * XW : (ch + 1) * XW, :] = total.astype(BF)
    near = [(lane % XW == r16 + di - 1) for di in range(3)]
    marks = [[(near[di] & (lane // XW == q)).astype(F32) for di in range(3)] for q in range(8)]
    for block in range(CH // 8):
        for dj in range(3):
            total = jnp.zeros((XW, 128), F32)
            for q in range(8):
                for di in range(3):
                    total = total + marks[q][di] * second[block * 8 + q, di * 3 + dj]
            k_out[dj * XW : (dj + 1) * XW, block * 128 : (block + 1) * 128] = total.astype(BF)

    flat[...] = sino[...].astype(F32).reshape(ANGLES * 16, 128)
    for r in range(2):
        rows_r = jnp.concatenate(
            [flat[pl.ds(2 * c + r, ANGLES, stride=16), :] for c in range(W // 128)], axis=1
        ).astype(BF)
        both = jnp.concatenate([rows_r, rows_r], axis=0)
        spread = jnp.dot(weights, both, preferred_element_type=F32)
        picture = jnp.zeros((XW, W), F32)
        for s in range(SHIFTS):
            picture = picture + shifted(spread[s * XW : (s + 1) * XW], s - SPREAD)
        rounded = picture.astype(BF).astype(F32)
        stack = jnp.concatenate([shifted(rounded, dj - 1) for dj in range(3)], axis=0).astype(BF)
        hidden = jnp.dot(k_in[:, : 3 * XW], stack, preferred_element_type=F32)
        hidden = jnp.maximum(hidden, 0.0).astype(BF)
        extra = jnp.dot(k_out[...], hidden, preferred_element_type=F32)
        for dj in range(3):
            picture = picture + shifted(extra[dj * XW : (dj + 1) * XW], dj - 1)
        out[r] = picture


def body(patches, magnitudes, probe, owners, scan_rows, scan_cols, slab_rows, angle_tan, prior_in, prior_out):
    vmem = pl.BlockSpec(memory_space=pltpu.VMEM)
    smem = pl.BlockSpec(memory_space=pltpu.SMEM)
    hbm = pl.BlockSpec(memory_space=pl.ANY)
    dma = pltpu.SemaphoreType.DMA
    numbers = dft_table(SIDE)
    table = jnp.asarray(numbers).astype(BF)
    table_t = jnp.asarray(np.ascontiguousarray(numbers.T)).astype(BF)
    rows_x = TZ * STRIP

    sino = pl.pallas_call(
        fused_kernel,
        out_shape=jax.ShapeDtypeStruct((ANGLES, 16, 128), BF),
        in_specs=[smem, smem, smem, smem, hbm, hbm, hbm, hbm, hbm],
        out_specs=vmem,
        scratch_shapes=[pltpu.VMEM((2 * TX, SIDE, SIDE), BF)] * TZ
        + [pltpu.VMEM((first + 1, HALF, SIDE, SIDE), BF) for _, first, _ in CHAINS]
        + [
            pltpu.VMEM((COUNT, 2, SIDE, SIDE), BF),
            pltpu.VMEM((2, SIDE, SIDE), F32),
            pltpu.VMEM((2 * SIDE, 2 * SIDE), BF),
            pltpu.VMEM((2 * SIDE, 2 * SIDE), BF),
            pltpu.VMEM((8, 128), jnp.int32),
            pltpu.VMEM((TZ, 8, 128), jnp.int32),
            pltpu.SMEM((TZ, 8, 128), jnp.int32),
            pltpu.VMEM((2 * SIDE, COUNT * SIDE), F32),
            pltpu.VMEM((H, COUNT * SIDE), BF),
            pltpu.VMEM((COUNT * SIDE, W), BF),
            pltpu.VMEM((CHUNKS, TX, rows_x, WIDE), BF),
            pltpu.VMEM((CHUNKS, TX, rows_x, WIDE), BF),
            pltpu.VMEM((CHUNKS, rows_x, WIDE), F32),
            pltpu.VMEM((CHUNKS, TZ, STRIP, WIDE), BF),
            pltpu.VMEM((CHUNKS, TZ, STRIP, WIDE), BF),
            pltpu.VMEM((ANGLES, 16, 128), BF),
            pltpu.VMEM((ANGLES, 16, 128), BF),
            pltpu.VMEM((ANGLES, 16, 128), BF),
            dma((12,)),
            dma((TZ, TX)),
            dma((TZ, TX)),
            dma((4, 5)),
            dma((4, 5)),
            dma((TZ,)),
            dma((TZ,)),
            dma,
            dma((CHUNKS, TX)),
            dma((CHUNKS, TX)),
            dma((CHUNKS, TZ)),
            dma((CHUNKS, TZ)),
            dma((ANGLES,)),
            dma((ANGLES,)),
        ],
        compiler_params=pltpu.CompilerParams(
            collective_id=0, has_side_effects=True, vmem_limit_bytes=60 * 1024 * 1024
        ),
        name="frames_to_slabs",
    )(
        owners.reshape(1, COUNT), scan_rows, scan_cols, slab_rows, patches[0], magnitudes[0], probe, table, table_t
    )

    volume = pl.pallas_call(
        slab_kernel,
        out_shape=jax.ShapeDtypeStruct((2, XW, W), F32),
        in_specs=[smem, smem, vmem, vmem],
        out_specs=vmem,
        scratch_shapes=[
            pltpu.VMEM((ANGLES * 16, 128), F32),
            pltpu.VMEM((CH * XW, 128), BF),
            pltpu.VMEM((3 * XW, CH * XW), BF),
        ],
        compiler_params=pltpu.CompilerParams(vmem_limit_bytes=48 * 1024 * 1024),
        name="slabs",
    )(
        prior_in.astype(F32).reshape(CH, 9),
        prior_out.astype(F32).reshape(CH, 9),
        angle_tan.reshape(1, ANGLES),
        sino,
    )
    return volume[None]


def solution(mesh):
    placed = (
        P("angle", "tile", None, None, None),
        P("angle", "tile", None, None),
        P(),
        P("angle", "tile", None),
        P("angle", "tile"),
        P("angle", "tile"),
        P("tile", None),
        P(),
        P(),
        P(),
    )
    return jax.shard_map(
        body, mesh=mesh, in_specs=placed, out_specs=P("tile", "angle", None, None), check_vma=False
    )
```

```python
import functools
import math

import jax
import jax.numpy as jnp
import numpy as np
from jax import lax
from jax.experimental import pallas as pl
from jax.experimental.pallas import tpu as pltpu
from jax.sharding import PartitionSpec as P

H = 512
W = 1024
XW = 16
CH = 16
SIDE = 128
COUNT = 8
TX = 4
TZ = 8
TILES = TX * TZ
ANGLES = 16
STRIP = H // TILES
SPREAD = 4
SHIFTS = 2 * SPREAD + 1
HALF = COUNT // 2
CHUNKS = 3
WIDE = W // (CHUNKS + 1)
AHEAD = 6
PARTS = 2
LINES = SIDE // PARTS
ORDER = ((4, 0), (4, 1), (3, 0), (-3, 0), (3, 1), (-3, 1), (2, 0), (-2, 0), (2, 1), (-2, 1), (1, 0), (-1, 0), (1, 1), (-1, 1), (0, 0), (0, 1))
CHAINS = ((1, 4, 0), (-1, 3, 0), (1, 3, HALF), (-1, 4, HALF))
MESH = pl.DeviceIdType.MESH
BF = jnp.bfloat16
F32 = jnp.float32


def dft_table(side):
    index = np.arange(side)
    phase = ((index[:, None] * index[None, :]) % side).astype(np.float32)
    phase = phase * np.float32(2.0 * math.pi / side)
    scale = np.float32(1.0 / math.sqrt(side))
    real = np.cos(phase) * scale
    imag = -np.sin(phase) * scale
    upper = np.concatenate([real, imag], axis=1)
    lower = np.concatenate([-imag, real], axis=1)
    return np.concatenate([upper, lower], axis=0).astype(np.float32)


def shifted(values, step):
    if step == 0:
        return values
    lane = lax.broadcasted_iota(jnp.int32, values.shape, 1) + step
    rolled = pltpu.roll(values, (-step) % W, 1)
    return jnp.where((lane >= 0) & (lane < W), rolled, 0.0)


def fused_kernel(
    owners, rows, cols, lengths, tangents, patches, mags, probe, table, table_t, first, second, out,
    f0, f1, f2, f3, f4, f5, f6, f7, f8, f9, f10, f11, f12, f13, f14, f15, c0, c1, c2, c3,
    waves, light, fwd, fwd_t, one_in, one_out, ids_out, ids_in, ids_s, spec, hot, placed, stage, from_x, mine, part,
    from_z, stage_b, from_zb, part_b, from_xb, sel, pieces, sino, flat, weights, k_in, k_out,
    loc, xs, xr, cs, cr, is_, ir, ls, sxs, sxr, szs, szr, bzs, bzr, bxs, bxr, as_, ar,
):
    frames = (f0, f1, f2, f3, f4, f5, f6, f7, f8, f9, f10, f11, f12, f13, f14, f15)
    chains = (c0, c1, c2, c3)
    a = lax.axis_index("angle")
    me = lax.axis_index("tile")
    x = me // TZ
    z = lax.rem(me, TZ)
    rows_x = TZ * STRIP

    def at_x(i):
        return lax.rem(x + i, TX) * TZ + z

    def at_z(i):
        return x * TZ + lax.rem(z + i + TZ, TZ)

    local = [
        pltpu.make_async_copy(patches, waves, loc.at[16]),
        pltpu.make_async_copy(table, fwd, loc.at[17]),
        pltpu.make_async_copy(table_t, fwd_t, loc.at[18]),
        pltpu.make_async_copy(probe, light, loc.at[19]),
        pltpu.make_async_copy(first, one_in, loc.at[20]),
        pltpu.make_async_copy(second, one_out, loc.at[21]),
    ]
    for copy in local:
        copy.start()

    def source_z(d):
        return lax.rem(z + d + TZ, TZ)

    def held(q):
        return frames[q].at[pl.ds(x * 2, 2)]

    def own_frames(q):
        d, h = ORDER[q]
        return pltpu.make_async_copy(
            mags.at[pl.ds((x * TZ + source_z(d)) * 2, 2), pl.ds(h * LINES, LINES)], held(q), loc.at[q]
        )

    for q in range(len(ORDER)):
        own_frames(q).start()

    barrier = pltpu.get_barrier_semaphore()
    for i in range(1, TX):
        pl.semaphore_signal(barrier, inc=1, device_id=(a, at_x(i)), device_id_type=MESH)
    for i in range(1, TZ):
        pl.semaphore_signal(barrier, inc=1, device_id=(a, at_z(i)), device_id_type=MESH)

    def greet(i, c):
        pl.semaphore_signal(barrier, inc=1, device_id=(lax.rem(a + i, ANGLES), me), device_id_type=MESH)
        return c

    lax.fori_loop(1, ANGLES, greet, 0)

    mine_ids = [owners[0, k] for k in range(COUNT)]
    lane = lax.broadcasted_iota(jnp.int32, (8, 128), 1)
    vector = jnp.zeros((8, 128), jnp.int32)
    for k in range(COUNT):
        vector = jnp.where(lane == k, mine_ids[k], vector)
    ids_out[...] = vector
    pl.semaphore_wait(barrier, TX + TZ + ANGLES - 3)

    def copy_ids(i):
        return pltpu.make_async_remote_copy(
            src_ref=ids_out, dst_ref=ids_in.at[i], send_sem=is_.at[i], recv_sem=ir.at[i],
            device_id=(a, at_z(i)), device_id_type=MESH,
        )

    for i in (4, 3, 5, 2, 6, 1, 7):
        copy_ids(i).start()

    def copy_x(q, i):
        d, h = ORDER[q]
        peer = at_x(i)
        return pltpu.make_async_remote_copy(
            src_ref=mags.at[pl.ds(((peer // TZ) * TZ + source_z(d)) * 2, 2), pl.ds(h * LINES, LINES)],
            dst_ref=held(q),
            send_sem=xs.at[q, i], recv_sem=xr.at[q, i],
            device_id=(a, peer), device_id_type=MESH,
        )

    def start_x(q):
        for i in (2, 1, 3):
            copy_x(q, i).start()

    for q in range(AHEAD):
        start_x(q)

    row_id = lax.broadcasted_iota(jnp.int32, (16, 128), 0)
    lane_id = lax.broadcasted_iota(jnp.int32, (16, 128), 1)
    within = row_id % 2
    same = (row_id // 2) == (lane_id // 16)
    place = lane_id % 16 - within
    begin = jnp.int32(0)
    for b in range(ANGLES):
        length = lengths[0, b]
        hit = same & (place == begin) & (within < length)
        sel[b] = hit.astype(F32).astype(BF)
        begin = begin + length
    gap = lax.broadcasted_iota(jnp.int32, (H, 128), 0) - lax.broadcasted_iota(jnp.int32, (H, 128), 1)
    for k in range(COUNT):
        hot[:, k * SIDE : (k + 1) * SIDE] = (gap == rows[0, k]).astype(F32).astype(BF)

    pair = 2

    def stack(values):
        return jnp.concatenate(
            [
                jnp.concatenate(
                    [values[j * SIDE : (j + 1) * SIDE, p * SIDE : (p + 1) * SIDE] for j in range(pair)], axis=1
                )
                for p in range(2)
            ],
            axis=0,
        )

    for copy in local:
        copy.wait()
    for g in range(COUNT // pair):
        joined = jnp.concatenate(
            [jnp.concatenate([waves[k, 0], waves[k, 1]], axis=1) for k in range(g * pair, (g + 1) * pair)], axis=0
        )
        half = jnp.dot(joined, fwd[...], preferred_element_type=F32).astype(BF)
        spec[:, g * pair * SIDE : (g + 1) * pair * SIDE] = jnp.dot(
            fwd_t[...], stack(half), preferred_element_type=F32
        )

    count = SHIFTS * XW
    row = lax.broadcasted_iota(jnp.int32, (count, ANGLES), 0)
    offset = (row % XW).astype(F32) - (XW - 1) / 2.0
    shift = (row // XW).astype(F32) - float(SPREAD)
    angle_lane = lax.broadcasted_iota(jnp.int32, (count, ANGLES), 1)
    tangent = jnp.zeros((count, ANGLES), F32)
    for k in range(ANGLES):
        tangent = jnp.where(angle_lane == k, tangents[k], tangent)
    weight = jnp.maximum(1.0 - jnp.abs(offset * tangent - shift), 0.0) * (1.0 / ANGLES)
    high = weight.astype(BF)
    low = (weight - high.astype(F32)).astype(BF)
    weights[...] = jnp.concatenate([high, low], axis=1)

    channels = CH * XW
    spread_ch = (
        lax.broadcasted_iota(jnp.int32, (CH, channels), 1) // XW == lax.broadcasted_iota(jnp.int32, (CH, channels), 0)
    )
    spread_ch = spread_ch.astype(F32).astype(BF)
    r16 = lax.broadcasted_iota(jnp.int32, (XW, channels), 0)
    l16 = lax.broadcasted_iota(jnp.int32, (XW, channels), 1) % XW
    first_taps = [jnp.dot(one_in[0, di], spread_ch, preferred_element_type=F32) for di in range(3)]
    second_taps = [jnp.dot(one_out[0, di], spread_ch, preferred_element_type=F32) for di in range(3)]
    turned = []
    for dj in range(3):
        total_in = jnp.zeros((XW, channels), F32)
        total_out = jnp.zeros((XW, channels), F32)
        for di in range(3):
            total_in = total_in + jnp.where(r16 == l16 + di - 1, first_taps[di][dj : dj + 1, :], 0.0)
            total_out = total_out + jnp.where(l16 == r16 + di - 1, second_taps[di][dj : dj + 1, :], 0.0)
        turned.append(total_in)
        k_out[dj * XW : (dj + 1) * XW, :] = total_out.astype(BF)
    turned = jnp.concatenate(turned + [jnp.zeros((128 - 3 * XW, channels), F32)], axis=0)
    k_in[...] = jnp.transpose(turned).astype(BF)

    for i in (1, 7, 2, 6, 3, 5, 4):
        copy_ids(i).wait_recv()
    to_scalar = pltpu.make_async_copy(ids_in, ids_s, ls)
    to_scalar.start()
    to_scalar.wait()

    def chosen(q):
        d, h = ORDER[q]
        ids = mine_ids if d == 0 else [ids_s[(-d) % TZ, 0, k] for k in range(COUNT)]

        def one(k):
            rank = jnp.int32(0)
            for j in range(k):
                rank = rank + jnp.where(ids[j] == ids[k], 1, 0).astype(jnp.int32)
            return (ids[k] & 7) == z, frames[q][((ids[k] >> 3) & 3) * 2 + (rank & 1)]

        return one

    def copy_chain(c, h, level):
        step = CHAINS[c][0]
        return pltpu.make_async_remote_copy(
            src_ref=chains[c].at[h, level], dst_ref=chains[c].at[h, level - 1],
            send_sem=cs.at[c, h, level], recv_sem=cr.at[c, h, level - 1],
            device_id=(a, at_z(step)), device_id_type=MESH,
        )

    for q in range(len(ORDER)):
        if q + AHEAD < len(ORDER):
            start_x(q + AHEAD)
        own_frames(q).wait()
        for i in (1, 3, 2):
            copy_x(q, i).wait_recv()
        d, h = ORDER[q]
        if d == 0:
            continue
        pick = chosen(q)
        for c in range(4):
            step, top, base = CHAINS[c]
            level = 4 if d == 4 else step * d
            if level < 1 or level > top:
                continue
            if level < top:
                copy_chain(c, h, level + 1).wait_recv()
            for k in range(HALF):
                hit, frame = pick(base + k)
                before = chains[c][h, level, k] if level < top else jnp.zeros((LINES, SIDE), BF)
                chains[c][h, level, k] = jnp.where(hit, frame, before)
            copy_chain(c, h, level).start()
    for h in range(PARTS):
        for c in range(4):
            copy_chain(c, h, 1).wait_recv()
    picks = [chosen(ORDER.index((0, h))) for h in range(PARTS)]

    for g in range(COUNT // pair):
        ks = [g * pair + j for j in range(pair)]
        measured = []
        for k in ks:
            two = (0, 1) if k < HALF else (2, 3)
            halves = []
            for h in range(PARTS):
                hit, frame = picks[h](k)
                came = chains[two[0]][h, 0, k % HALF] + chains[two[1]][h, 0, k % HALF]
                halves.append(jnp.where(hit, frame, came).astype(F32))
            measured.append(jnp.concatenate(halves, axis=0))
        part_g = slice(g * pair * SIDE, (g + 1) * pair * SIDE)
        real = spec[:SIDE, part_g]
        imag = spec[SIDE:, part_g]
        factor = jnp.concatenate(measured, axis=1) * lax.rsqrt(real * real + imag * imag + 0.25)
        real = (real * factor).astype(BF)
        imag = (imag * factor).astype(BF)
        target = jnp.concatenate(
            [
                jnp.concatenate([real[:, j * SIDE : (j + 1) * SIDE], imag[:, j * SIDE : (j + 1) * SIDE]], axis=1)
                for j in range(pair)
            ],
            axis=0,
        )
        back = jnp.dot(target, fwd_t[...], preferred_element_type=F32).astype(BF)
        result = jnp.dot(fwd[...], stack(back), preferred_element_type=F32)
        for j in range(pair):
            k = ks[j]
            at = slice(j * SIDE, (j + 1) * SIDE)
            contrib = (light[0] * result[SIDE:, at] - light[1] * result[:SIDE, at]) * 0.25
            col = cols[0, k]
            low = col >> 7
            wide = jnp.concatenate([contrib, jnp.zeros((SIDE, SIDE), F32)], axis=1)
            wide = pltpu.roll(wide, col & 127, 1).astype(BF)
            left = wide[:, :SIDE]
            right = wide[:, SIDE:]
            none = jnp.zeros((SIDE, SIDE), BF)
            for b in range(W // SIDE):
                placed[k * SIDE : (k + 1) * SIDE, b * SIDE : (b + 1) * SIDE] = jnp.where(
                    low == b, left, jnp.where(low + 1 == b, right, none)
                )

    def copy_s(n, i):
        return pltpu.make_async_remote_copy(
            src_ref=stage.at[n, i], dst_ref=from_x.at[n, i], send_sem=sxs.at[n, i], recv_sem=sxr.at[n, i],
            device_id=(a, at_x(i)), device_id_type=MESH,
        )

    def canvas_of(n, i):
        at = pl.ds(pl.multiple_of(lax.rem(x + i, TX) * rows_x, rows_x), rows_x)
        return jnp.dot(hot[at, :], placed[:, n * WIDE : (n + 1) * WIDE], preferred_element_type=F32)

    def copy_zb(i):
        return pltpu.make_async_remote_copy(
            src_ref=stage_b.at[lax.rem(z + i, TZ)], dst_ref=from_zb.at[i], send_sem=bzs.at[i], recv_sem=bzr.at[i],
            device_id=(a, at_z(i)), device_id_type=MESH,
        )

    def copy_xb(i):
        return pltpu.make_async_remote_copy(
            src_ref=part_b.at[lax.rem(x + i, TX)], dst_ref=from_xb.at[i], send_sem=bxs.at[i], recv_sem=bxr.at[i],
            device_id=(a, at_x(i)), device_id_type=MESH,
        )

    last = jnp.dot(hot[...], placed[:, CHUNKS * WIDE :], preferred_element_type=F32).astype(BF)
    for j in range(TZ):
        for k in range(TX):
            stage_b[j, k] = last[(k * TZ + j) * STRIP : (k * TZ + j + 1) * STRIP]
    for i in (4, 3, 5, 2, 6, 1, 7):
        copy_zb(i).start()

    for n in range(CHUNKS):
        for i in (2, 1, 3):
            stage[n, i] = canvas_of(n, i).astype(BF)
            copy_s(n, i).start()
        mine[n] = canvas_of(n, 0)

    def copy_z(n, i):
        return pltpu.make_async_remote_copy(
            src_ref=part.at[n, lax.rem(z + i, TZ)], dst_ref=from_z.at[n, i],
            send_sem=szs.at[n, i], recv_sem=szr.at[n, i],
            device_id=(a, at_z(i)), device_id_type=MESH,
        )

    for n in range(CHUNKS):
        total = mine[n]
        for i in (1, 3, 2):
            copy_s(n, i).wait_recv()
            total = total + from_x[n, i].astype(F32)
        total = total.astype(BF)
        for j in range(TZ):
            part[n, j] = total[j * STRIP : (j + 1) * STRIP]
        for i in (4, 3, 5, 2, 6, 1, 7):
            copy_z(n, i).start()
        if n == 0:
            total = stage_b[z].astype(F32)
            for i in (1, 7, 2, 6, 3, 5, 4):
                copy_zb(i).wait_recv()
                total = total + from_zb[i].astype(F32)
            part_b[...] = total.astype(BF)
            for i in (2, 1, 3):
                copy_xb(i).start()

    blocks = []
    for n in range(CHUNKS + 1):
        if n < CHUNKS:
            strip = part[n, z].astype(F32)
            for i in (1, 7, 2, 6, 3, 5, 4):
                copy_z(n, i).wait_recv()
                strip = strip + from_z[n, i].astype(F32)
        else:
            strip = part_b[x].astype(F32)
            for i in (1, 3, 2):
                copy_xb(i).wait_recv()
                strip = strip + from_xb[i].astype(F32)
        strip = strip.astype(BF)
        blocks += [strip[:, c * 128 : (c + 1) * 128] for c in range(WIDE // 128)]
    picked = jnp.dot(
        sel[...].reshape(ANGLES * 16, 128), jnp.concatenate(blocks, axis=0), preferred_element_type=F32
    )
    pieces[...] = picked.astype(BF).reshape(ANGLES, 16, 128)

    def copy_a(i):
        peer = lax.rem(a + i, ANGLES)
        return pltpu.make_async_remote_copy(
            src_ref=pieces.at[peer], dst_ref=sino.at[a], send_sem=as_.at[i], recv_sem=ar.at[i],
            device_id=(peer, me), device_id_type=MESH,
        )

    def start_a(i, c):
        copy_a(i).start()
        return c

    lax.fori_loop(1, ANGLES, start_a, 0)
    sino[a] = pieces[a]

    for i in range(1, TZ):
        copy_ids(i).wait_send()
    for q in range(len(ORDER)):
        for i in range(1, TX):
            copy_x(q, i).wait_send()
    for c in range(4):
        for h in range(PARTS):
            for level in range(1, CHAINS[c][1] + 1):
                copy_chain(c, h, level).wait_send()
    for i in range(1, TZ):
        copy_zb(i).wait_send()
    for i in range(1, TX):
        copy_xb(i).wait_send()
    for n in range(CHUNKS):
        for i in range(1, TX):
            copy_s(n, i).wait_send()
        for i in range(1, TZ):
            copy_z(n, i).wait_send()

    def finish_a(i, c):
        source = lax.rem(a - i + ANGLES, ANGLES)
        pltpu.make_async_remote_copy(
            src_ref=pieces.at[source], dst_ref=sino.at[source], send_sem=as_.at[i], recv_sem=ar.at[i],
            device_id=(source, me), device_id_type=MESH,
        ).wait_recv()
        return c

    lax.fori_loop(1, ANGLES, finish_a, 0)

    def sent_a(i, c):
        copy_a(i).wait_send()
        return c

    lax.fori_loop(1, ANGLES, sent_a, 0)

    flat[...] = sino[...].astype(F32).reshape(ANGLES * 16, 128)
    for r in range(2):
        rows_r = jnp.concatenate(
            [flat[pl.ds(2 * c + r, ANGLES, stride=16), :] for c in range(W // 128)], axis=1
        ).astype(BF)
        both = jnp.concatenate([rows_r, rows_r], axis=0)
        spread = jnp.dot(weights[...], both, preferred_element_type=F32)
        picture = jnp.zeros((XW, W), F32)
        for s in range(SHIFTS):
            picture = picture + shifted(spread[s * XW : (s + 1) * XW], s - SPREAD)
        rounded = picture.astype(BF).astype(F32)
        stack = jnp.concatenate([shifted(rounded, dj - 1) for dj in range(3)], axis=0).astype(BF)
        hidden = jnp.dot(k_in[:, : 3 * XW], stack, preferred_element_type=F32)
        hidden = jnp.maximum(hidden, 0.0).astype(BF)
        extra = jnp.dot(k_out[...], hidden, preferred_element_type=F32)
        for dj in range(3):
            picture = picture + shifted(extra[dj * XW : (dj + 1) * XW], dj - 1)
        out[r] = picture


def body(patches, magnitudes, probe, owners, scan_rows, scan_cols, slab_rows, angle_tan, prior_in, prior_out):
    vmem = pl.BlockSpec(memory_space=pltpu.VMEM)
    smem = pl.BlockSpec(memory_space=pltpu.SMEM)
    hbm = pl.BlockSpec(memory_space=pltpu.HBM)
    dma = pltpu.SemaphoreType.DMA
    stay = functools.partial(pltpu.with_memory_space_constraint, memory_space=pltpu.HBM)
    numbers = dft_table(SIDE)
    table = jnp.asarray(numbers).astype(BF)
    table_t = jnp.asarray(np.ascontiguousarray(numbers.T)).astype(BF)
    rows_x = TZ * STRIP

    volume = pl.pallas_call(
        fused_kernel,
        out_shape=jax.ShapeDtypeStruct((2, XW, W), F32),
        in_specs=[smem, smem, smem, smem, smem, hbm, hbm, hbm, hbm, hbm, hbm, hbm],
        out_specs=vmem,
        scratch_shapes=[pltpu.VMEM((2 * TX, LINES, SIDE), BF)] * (PARTS * TZ)
        + [pltpu.VMEM((PARTS, top + 1, HALF, LINES, SIDE), BF) for _, top, _ in CHAINS]
        + [
            pltpu.VMEM((COUNT, 2, SIDE, SIDE), BF),
            pltpu.VMEM((2, SIDE, SIDE), F32),
            pltpu.VMEM((2 * SIDE, 2 * SIDE), BF),
            pltpu.VMEM((2 * SIDE, 2 * SIDE), BF),
            pltpu.VMEM((1, 3, 3, CH), BF),
            pltpu.VMEM((1, 3, 3, CH), BF),
            pltpu.VMEM((8, 128), jnp.int32),
            pltpu.VMEM((TZ, 8, 128), jnp.int32),
            pltpu.SMEM((TZ, 8, 128), jnp.int32),
            pltpu.VMEM((2 * SIDE, COUNT * SIDE), F32),
            pltpu.VMEM((H, COUNT * SIDE), BF),
            pltpu.VMEM((COUNT * SIDE, W), BF),
            pltpu.VMEM((CHUNKS, TX, rows_x, WIDE), BF),
            pltpu.VMEM((CHUNKS, TX, rows_x, WIDE), BF),
            pltpu.VMEM((CHUNKS, rows_x, WIDE), F32),
            pltpu.VMEM((CHUNKS, TZ, STRIP, WIDE), BF),
            pltpu.VMEM((CHUNKS, TZ, STRIP, WIDE), BF),
            pltpu.VMEM((TZ, TX, STRIP, WIDE), BF),
            pltpu.VMEM((TZ, TX, STRIP, WIDE), BF),
            pltpu.VMEM((TX, STRIP, WIDE), BF),
            pltpu.VMEM((TX, STRIP, WIDE), BF),
            pltpu.VMEM((ANGLES, 16, 128), BF),
            pltpu.VMEM((ANGLES, 16, 128), BF),
            pltpu.VMEM((ANGLES, 16, 128), BF),
            pltpu.VMEM((ANGLES * 16, 128), F32),
            pltpu.VMEM((SHIFTS * XW, 2 * ANGLES), BF),
            pltpu.VMEM((CH * XW, 128), BF),
            pltpu.VMEM((3 * XW, CH * XW), BF),
            dma((22,)),
            dma((16, TX)),
            dma((16, TX)),
            dma((4, PARTS, 5)),
            dma((4, PARTS, 5)),
            dma((TZ,)),
            dma((TZ,)),
            dma,
            dma((CHUNKS, TX)),
            dma((CHUNKS, TX)),
            dma((CHUNKS, TZ)),
            dma((CHUNKS, TZ)),
            dma((TZ,)),
            dma((TZ,)),
            dma((TX,)),
            dma((TX,)),
            dma((ANGLES,)),
            dma((ANGLES,)),
        ],
        compiler_params=pltpu.CompilerParams(
            collective_id=0, has_side_effects=True, vmem_limit_bytes=32 * 1024 * 1024
        ),
        name="frames_to_volume",
    )(
        stay(owners.reshape(1, COUNT)), stay(scan_rows), stay(scan_cols), stay(slab_rows), stay(angle_tan), stay(patches[0]), stay(magnitudes[0]),
        stay(probe), stay(table), stay(table_t), stay(prior_in.transpose(1, 2, 3, 0)),
        stay(prior_out.transpose(0, 2, 3, 1)),
    )
    return volume[None]


def solution(mesh):
    placed = (
        P("angle", "tile", None, None, None),
        P("angle", "tile", None, None),
        P(),
        P("angle", "tile", None),
        P("angle", "tile"),
        P("angle", "tile"),
        P("tile", None),
        P(),
        P(),
        P(),
    )
    return jax.shard_map(
        body, mesh=mesh, in_specs=placed, out_specs=P("tile", "angle", None, None), check_vma=False
    )
```

```python
import functools
import math

import jax
import jax.numpy as jnp
import numpy as np
from jax import lax
from jax.experimental import pallas as pl
from jax.experimental.pallas import tpu as pltpu
from jax.sharding import PartitionSpec as P

H = 512
W = 1024
XW = 16
CH = 16
SIDE = 128
COUNT = 8
TX = 4
TZ = 8
TILES = TX * TZ
ANGLES = 16
STRIP = H // TILES
SPREAD = 4
SHIFTS = 2 * SPREAD + 1
HALF = COUNT // 2
TOP = TZ // 2
CHUNKS = 2
LAST = 256
WIDE = (W - LAST) // CHUNKS
AHEAD = 6
PARTS = 2
LINES = SIDE // PARTS
ORDER = ((4, 0), (4, 1), (3, 0), (-3, 0), (3, 1), (-3, 1), (2, 0), (-2, 0), (2, 1), (-2, 1), (1, 0), (-1, 0), (1, 1), (-1, 1), (0, 0), (0, 1))
CHAINS = ((1, 0), (-1, HALF))
MESH = pl.DeviceIdType.MESH
BF = jnp.bfloat16
F32 = jnp.float32


def dft_table(side):
    index = np.arange(side)
    phase = ((index[:, None] * index[None, :]) % side).astype(np.float32)
    phase = phase * np.float32(2.0 * math.pi / side)
    scale = np.float32(1.0 / math.sqrt(side))
    real = np.cos(phase) * scale
    imag = -np.sin(phase) * scale
    upper = np.concatenate([real, imag], axis=1)
    lower = np.concatenate([-imag, real], axis=1)
    return np.concatenate([upper, lower], axis=0).astype(np.float32)


def shifted(values, step):
    if step == 0:
        return values
    lane = lax.broadcasted_iota(jnp.int32, values.shape, 1) + step
    rolled = pltpu.roll(values, (-step) % W, 1)
    return jnp.where((lane >= 0) & (lane < W), rolled, 0.0)


def fused_kernel(
    owners_in, rows_in, cols_in, lengths_in, tangents_in, patches, mags, probe, table, table_t, first, second, out,
    f0, f1, f2, f3, f4, f5, f6, f7, f8, f9, f10, f11, f12, f13, f14, f15, c0, c1,
    owners, rows, cols, lengths, tangents, waves, light, fwd, fwd_t, one_in, one_out, ids_out, ids_in, spec, hot, placed, stage, from_x, part,
    from_z, stage_b, from_zb, part_b, from_xb, sel, pieces, sino, flat, weights, k_in, k_out,
    loc, xs, xr, cs, cr, is_, ir, sxs, sxr, szs, szr, bzs, bzr, bxs, bxr, as_, ar,
):
    frames = (f0, f1, f2, f3, f4, f5, f6, f7, f8, f9, f10, f11, f12, f13, f14, f15)
    chains = (c0, c1)
    a = lax.axis_index("angle")
    me = lax.axis_index("tile")
    x = me // TZ
    z = lax.rem(me, TZ)
    rows_x = TZ * STRIP

    def at_x(i):
        return lax.rem(x + i, TX) * TZ + z

    def at_z(i):
        return x * TZ + lax.rem(z + i + TZ, TZ)

    barrier = pltpu.get_barrier_semaphore()
    for i in (2, 1, 3):
        pl.semaphore_signal(barrier, inc=1, device_id=(a, at_x(i)), device_id_type=MESH)
    for i in (4, 3, 5, 2, 6, 1, 7):
        pl.semaphore_signal(barrier, inc=1, device_id=(a, at_z(i)), device_id_type=MESH)

    def greet(i, c):
        pl.semaphore_signal(barrier, inc=1, device_id=(lax.rem(a + i, ANGLES), me), device_id_type=MESH)
        return c

    lax.fori_loop(1, ANGLES, greet, 0)

    small = [
        pltpu.make_async_copy(a_ref, b_ref, loc.at[22 + n])
        for n, (a_ref, b_ref) in enumerate(
            (
                (owners_in, owners), (rows_in, rows), (cols_in, cols), (lengths_in, lengths), (tangents_in, tangents),
            )
        )
    ]
    for copy in small:
        copy.start()
    local = [
        pltpu.make_async_copy(patches, waves, loc.at[16]),
        pltpu.make_async_copy(table, fwd, loc.at[17]),
        pltpu.make_async_copy(table_t, fwd_t, loc.at[18]),
        pltpu.make_async_copy(probe, light, loc.at[19]),
        pltpu.make_async_copy(first, one_in, loc.at[20]),
        pltpu.make_async_copy(second, one_out, loc.at[21]),
    ]
    for copy in local:
        copy.start()

    def source_z(d):
        return lax.rem(z + d + TZ, TZ)

    def held(q):
        return frames[q].at[pl.ds(x * 2, 2)]

    def own_frames(q):
        d, h = ORDER[q]
        return pltpu.make_async_copy(
            mags.at[pl.ds((x * TZ + source_z(d)) * 2, 2), pl.ds(h * LINES, LINES)], held(q), loc.at[q]
        )

    for q in range(len(ORDER)):
        own_frames(q).start()

    for copy in small:
        copy.wait()
    named = [owners[0, k] for k in range(COUNT)]
    mine_ids = []
    for k in range(COUNT):
        rank = jnp.int32(0)
        for j in range(k):
            rank = rank + jnp.where(named[j] == named[k], 1, 0).astype(jnp.int32)
        mine_ids.append((named[k] & 7) * 16 + ((named[k] >> 3) & 3) * 2 + (rank & 1))
    lane = lax.broadcasted_iota(jnp.int32, (8, 128), 1)
    vector = jnp.zeros((8, 128), jnp.int32)
    for k in range(COUNT):
        vector = jnp.where(lane == k, mine_ids[k], vector)
    ids_out[...] = vector
    pl.semaphore_wait(barrier, TX + TZ + ANGLES - 3)

    def copy_ids(i):
        return pltpu.make_async_remote_copy(
            src_ref=ids_out, dst_ref=ids_in.at[i], send_sem=is_.at[i], recv_sem=ir.at[i],
            device_id=(a, at_z(i)), device_id_type=MESH,
        )

    for i in (4, 3, 5, 2, 6, 1, 7):
        copy_ids(i).start()

    def copy_x(q, i):
        d, h = ORDER[q]
        peer = at_x(i)
        return pltpu.make_async_remote_copy(
            src_ref=mags.at[pl.ds(((peer // TZ) * TZ + source_z(d)) * 2, 2), pl.ds(h * LINES, LINES)],
            dst_ref=held(q),
            send_sem=xs.at[q, i], recv_sem=xr.at[q, i],
            device_id=(a, peer), device_id_type=MESH,
        )

    def start_x(q):
        for i in (2, 1, 3):
            copy_x(q, i).start()

    for q in range(AHEAD):
        start_x(q)

    pair = 2

    def stack(values):
        return jnp.concatenate(
            [
                jnp.concatenate(
                    [values[j * SIDE : (j + 1) * SIDE, p * SIDE : (p + 1) * SIDE] for j in range(pair)], axis=1
                )
                for p in range(2)
            ],
            axis=0,
        )

    def slab_rows_of():
        row_id = lax.broadcasted_iota(jnp.int32, (16, 128), 0)
        lane_id = lax.broadcasted_iota(jnp.int32, (16, 128), 1)
        within = row_id % 2
        same = (row_id // 2) == (lane_id // 16)
        place = lane_id % 16 - within
        begin = jnp.int32(0)
        for b in range(ANGLES):
            length = lengths[0, b]
            hit = same & (place == begin) & (within < length)
            sel[b] = hit.astype(F32).astype(BF)
            begin = begin + length

    def row_places(ks):
        gap = lax.broadcasted_iota(jnp.int32, (H, 128), 0) - lax.broadcasted_iota(jnp.int32, (H, 128), 1)
        for k in ks:
            hot[:, k * SIDE : (k + 1) * SIDE] = (gap == rows[0, k]).astype(F32).astype(BF)

    def forward(gs):
        for g in gs:
            joined = jnp.concatenate(
                [jnp.concatenate([waves[k, 0], waves[k, 1]], axis=1) for k in range(g * pair, (g + 1) * pair)], axis=0
            )
            half = jnp.dot(joined, fwd[...], preferred_element_type=F32).astype(BF)
            spec[:, g * pair * SIDE : (g + 1) * pair * SIDE] = jnp.dot(
                fwd_t[...], stack(half), preferred_element_type=F32
            )

    def matrices():
        count = SHIFTS * XW
        row = lax.broadcasted_iota(jnp.int32, (count, ANGLES), 0)
        offset = (row % XW).astype(F32) - (XW - 1) / 2.0
        shift = (row // XW).astype(F32) - float(SPREAD)
        angle_lane = lax.broadcasted_iota(jnp.int32, (count, ANGLES), 1)
        tangent = jnp.zeros((count, ANGLES), F32)
        for k in range(ANGLES):
            tangent = jnp.where(angle_lane == k, tangents[k], tangent)
        weight = jnp.maximum(1.0 - jnp.abs(offset * tangent - shift), 0.0) * (1.0 / ANGLES)
        high = weight.astype(BF)
        low = (weight - high.astype(F32)).astype(BF)
        weights[...] = jnp.concatenate([high, low], axis=1)

        channels = CH * XW
        spread_ch = (
            lax.broadcasted_iota(jnp.int32, (CH, channels), 1) // XW == lax.broadcasted_iota(jnp.int32, (CH, channels), 0)
        )
        spread_ch = spread_ch.astype(F32).astype(BF)
        r16 = lax.broadcasted_iota(jnp.int32, (XW, channels), 0)
        l16 = lax.broadcasted_iota(jnp.int32, (XW, channels), 1) % XW
        first_taps = [jnp.dot(one_in[0, di], spread_ch, preferred_element_type=F32) for di in range(3)]
        second_taps = [jnp.dot(one_out[0, di], spread_ch, preferred_element_type=F32) for di in range(3)]
        turned = []
        for dj in range(3):
            total_in = jnp.zeros((XW, channels), F32)
            total_out = jnp.zeros((XW, channels), F32)
            for di in range(3):
                total_in = total_in + jnp.where(r16 == l16 + di - 1, first_taps[di][dj : dj + 1, :], 0.0)
                total_out = total_out + jnp.where(l16 == r16 + di - 1, second_taps[di][dj : dj + 1, :], 0.0)
            turned.append(total_in)
            k_out[dj * XW : (dj + 1) * XW, :] = total_out.astype(BF)
        turned = jnp.concatenate(turned + [jnp.zeros((128 - 3 * XW, channels), F32)], axis=0)
        k_in[...] = jnp.transpose(turned).astype(BF)

    def job(q):
        if q == 1:
            for copy in local:
                copy.wait()
            forward((0, 1))
        elif q == 3:
            forward((2, 3))
        elif q == 5:
            row_places(range(HALF))
        elif q == 7:
            row_places(range(HALF, COUNT))
        elif q == 9:
            matrices()
        elif q == 11:
            slab_rows_of()

    known = {0: mine_ids}

    def chosen(q):
        d, h = ORDER[q]
        if d not in known:
            came = (-d) % TZ
            copy_ids(came).wait_recv()
            known[d] = [ids_in[came, 0, k] for k in range(COUNT)]
        ids = known[d]

        def one(k):
            return (ids[k] >> 4) == z, frames[q][ids[k] & 7]

        return one

    def copy_chain(c, h, level):
        step, base = CHAINS[c]
        at = pl.ds(base, HALF) if level == TOP else pl.ds(0, COUNT)
        return pltpu.make_async_remote_copy(
            src_ref=chains[c].at[h, level, at], dst_ref=chains[c].at[h, level - 1, at],
            send_sem=cs.at[c, h, level], recv_sem=cr.at[c, h, level - 1],
            device_id=(a, at_z(step)), device_id_type=MESH,
        )

    for q in range(len(ORDER)):
        if q + AHEAD < len(ORDER):
            start_x(q + AHEAD)
        own_frames(q).wait()
        for i in (1, 3, 2):
            copy_x(q, i).wait_recv()
        d, h = ORDER[q]
        if d == 0:
            continue
        pick = chosen(q)
        for c in range(2):
            step, base = CHAINS[c]
            level = TOP if d == TOP else step * d
            if level < 1:
                continue
            if level < TOP:
                copy_chain(c, h, level + 1).wait_recv()
            for k in range(COUNT):
                here = base <= k < base + HALF
                if level == TOP and not here:
                    continue
                hit, frame = pick(k)
                came = level < TOP - 1 or (level == TOP - 1 and here)
                before = chains[c][h, level, k] if came else jnp.zeros((LINES, SIDE), BF)
                chains[c][h, level, k] = jnp.where(hit, frame, before)
            copy_chain(c, h, level).start()
        job(q)
    for h in range(PARTS):
        for c in range(2):
            copy_chain(c, h, 1).wait_recv()
    picks = [chosen(ORDER.index((0, h))) for h in range(PARTS)]

    for g in range(COUNT // pair):
        ks = [g * pair + j for j in range(pair)]
        measured = []
        for k in ks:
            halves = []
            for h in range(PARTS):
                hit, frame = picks[h](k)
                came = chains[0][h, 0, k] + chains[1][h, 0, k]
                halves.append(jnp.where(hit, frame, came).astype(F32))
            measured.append(jnp.concatenate(halves, axis=0))
        part_g = slice(g * pair * SIDE, (g + 1) * pair * SIDE)
        real = spec[:SIDE, part_g]
        imag = spec[SIDE:, part_g]
        factor = jnp.concatenate(measured, axis=1) * lax.rsqrt(real * real + imag * imag + 0.25)
        real = (real * factor).astype(BF)
        imag = (imag * factor).astype(BF)
        target = jnp.concatenate(
            [
                jnp.concatenate([real[:, j * SIDE : (j + 1) * SIDE], imag[:, j * SIDE : (j + 1) * SIDE]], axis=1)
                for j in range(pair)
            ],
            axis=0,
        )
        back = jnp.dot(target, fwd_t[...], preferred_element_type=F32).astype(BF)
        result = jnp.dot(fwd[...], stack(back), preferred_element_type=F32)
        for j in range(pair):
            k = ks[j]
            at = slice(j * SIDE, (j + 1) * SIDE)
            contrib = (light[0] * result[SIDE:, at] - light[1] * result[:SIDE, at]) * 0.25
            col = cols[0, k]
            low = col >> 7
            wide = jnp.concatenate([contrib, jnp.zeros((SIDE, SIDE), F32)], axis=1)
            wide = pltpu.roll(wide, col & 127, 1).astype(BF)
            left = wide[:, :SIDE]
            right = wide[:, SIDE:]
            none = jnp.zeros((SIDE, SIDE), BF)
            for b in range(W // SIDE):
                placed[k * SIDE : (k + 1) * SIDE, b * SIDE : (b + 1) * SIDE] = jnp.where(
                    low == b, left, jnp.where(low + 1 == b, right, none)
                )

    def copy_s(n, i):
        return pltpu.make_async_remote_copy(
            src_ref=stage.at[n, lax.rem(x + i, TX)], dst_ref=from_x.at[n, i],
            send_sem=sxs.at[n, i], recv_sem=sxr.at[n, i],
            device_id=(a, at_x(i)), device_id_type=MESH,
        )

    def canvas_of(n):
        return jnp.dot(hot[...], placed[:, n * WIDE : min(n * WIDE + WIDE, W)], preferred_element_type=F32).astype(BF)

    def copy_zb(i):
        return pltpu.make_async_remote_copy(
            src_ref=stage_b.at[lax.rem(z + i, TZ)], dst_ref=from_zb.at[i], send_sem=bzs.at[i], recv_sem=bzr.at[i],
            device_id=(a, at_z(i)), device_id_type=MESH,
        )

    def copy_xb(i):
        return pltpu.make_async_remote_copy(
            src_ref=part_b.at[lax.rem(x + i, TX)], dst_ref=from_xb.at[i], send_sem=bxs.at[i], recv_sem=bxr.at[i],
            device_id=(a, at_x(i)), device_id_type=MESH,
        )

    last = canvas_of(CHUNKS)
    for j in range(TZ):
        for k in range(TX):
            stage_b[j, k] = last[(k * TZ + j) * STRIP : (k * TZ + j + 1) * STRIP]
    for i in (4, 3, 5, 2, 6, 1, 7):
        copy_zb(i).start()

    for n in range(CHUNKS):
        whole = canvas_of(n)
        for j in range(TX):
            stage[n, j] = whole[j * rows_x : (j + 1) * rows_x]
        for i in (2, 1, 3):
            copy_s(n, i).start()

    def copy_z(n, i):
        return pltpu.make_async_remote_copy(
            src_ref=part.at[n, lax.rem(z + i, TZ)], dst_ref=from_z.at[n, i],
            send_sem=szs.at[n, i], recv_sem=szr.at[n, i],
            device_id=(a, at_z(i)), device_id_type=MESH,
        )

    for n in range(CHUNKS):
        total = stage[n, x].astype(F32)
        for i in (1, 3, 2):
            copy_s(n, i).wait_recv()
            total = total + from_x[n, i].astype(F32)
        total = total.astype(BF)
        for j in range(TZ):
            part[n, j] = total[j * STRIP : (j + 1) * STRIP]
        for i in (4, 3, 5, 2, 6, 1, 7):
            copy_z(n, i).start()
        if n == 0:
            total = stage_b[z].astype(F32)
            for i in (1, 7, 2, 6, 3, 5, 4):
                copy_zb(i).wait_recv()
                total = total + from_zb[i].astype(F32)
            part_b[...] = total.astype(BF)
            for i in (2, 1, 3):
                copy_xb(i).start()

    blocks = []
    for n in range(CHUNKS + 1):
        if n < CHUNKS:
            strip = part[n, z].astype(F32)
            for i in (1, 7, 2, 6, 3, 5, 4):
                copy_z(n, i).wait_recv()
                strip = strip + from_z[n, i].astype(F32)
        else:
            strip = part_b[x].astype(F32)
            for i in (1, 3, 2):
                copy_xb(i).wait_recv()
                strip = strip + from_xb[i].astype(F32)
        strip = strip.astype(BF)
        blocks += [strip[:, c * 128 : (c + 1) * 128] for c in range(strip.shape[1] // 128)]
    picked = jnp.dot(
        sel[...].reshape(ANGLES * 16, 128), jnp.concatenate(blocks, axis=0), preferred_element_type=F32
    )
    pieces[...] = picked.astype(BF).reshape(ANGLES, 16, 128)

    def copy_a(i):
        peer = lax.rem(a + i, ANGLES)
        return pltpu.make_async_remote_copy(
            src_ref=pieces.at[peer], dst_ref=sino.at[a], send_sem=as_.at[i], recv_sem=ar.at[i],
            device_id=(peer, me), device_id_type=MESH,
        )

    def start_a(i, c):
        copy_a(i).start()
        return c

    lax.fori_loop(1, ANGLES, start_a, 0)
    sino[a] = pieces[a]

    for i in range(1, TZ):
        copy_ids(i).wait_send()
    for q in range(len(ORDER)):
        for i in range(1, TX):
            copy_x(q, i).wait_send()
    for c in range(2):
        for h in range(PARTS):
            for level in range(1, TOP + 1):
                copy_chain(c, h, level).wait_send()
    for i in range(1, TZ):
        copy_zb(i).wait_send()
    for i in range(1, TX):
        copy_xb(i).wait_send()
    for n in range(CHUNKS):
        for i in range(1, TX):
            copy_s(n, i).wait_send()
        for i in range(1, TZ):
            copy_z(n, i).wait_send()

    def finish_a(i, c):
        source = lax.rem(a - i + ANGLES, ANGLES)
        pltpu.make_async_remote_copy(
            src_ref=pieces.at[source], dst_ref=sino.at[source], send_sem=as_.at[i], recv_sem=ar.at[i],
            device_id=(source, me), device_id_type=MESH,
        ).wait_recv()
        return c

    lax.fori_loop(1, ANGLES, finish_a, 0)

    flat[...] = sino[...].astype(F32).reshape(ANGLES * 16, 128)
    for r in range(2):
        rows_r = jnp.concatenate(
            [flat[pl.ds(2 * c + r, ANGLES, stride=16), :] for c in range(W // 128)], axis=1
        ).astype(BF)
        both = jnp.concatenate([rows_r, rows_r], axis=0)
        spread = jnp.dot(weights[...], both, preferred_element_type=F32)
        picture = jnp.zeros((XW, W), F32)
        for s in range(SHIFTS):
            picture = picture + shifted(spread[s * XW : (s + 1) * XW], s - SPREAD)
        rounded = picture.astype(BF).astype(F32)
        stack = jnp.concatenate([shifted(rounded, dj - 1) for dj in range(3)], axis=0).astype(BF)
        hidden = jnp.dot(k_in[:, : 3 * XW], stack, preferred_element_type=F32)
        hidden = jnp.maximum(hidden, 0.0).astype(BF)
        extra = jnp.dot(k_out[...], hidden, preferred_element_type=F32)
        for dj in range(3):
            picture = picture + shifted(extra[dj * XW : (dj + 1) * XW], dj - 1)
        out[r] = picture

    def sent_a(i, c):
        copy_a(i).wait_send()
        return c

    lax.fori_loop(1, ANGLES, sent_a, 0)


def body(patches, magnitudes, probe, owners, scan_rows, scan_cols, slab_rows, angle_tan, prior_in, prior_out):
    vmem = pl.BlockSpec(memory_space=pltpu.VMEM)
    hbm = pl.BlockSpec(memory_space=pltpu.HBM)
    dma = pltpu.SemaphoreType.DMA
    stay = functools.partial(pltpu.with_memory_space_constraint, memory_space=pltpu.HBM)
    numbers = dft_table(SIDE)
    table = jnp.asarray(numbers).astype(BF)
    table_t = jnp.asarray(np.ascontiguousarray(numbers.T)).astype(BF)
    rows_x = TZ * STRIP

    volume = pl.pallas_call(
        fused_kernel,
        out_shape=jax.ShapeDtypeStruct((2, XW, W), F32),
        in_specs=[hbm, hbm, hbm, hbm, hbm, hbm, hbm, hbm, hbm, hbm, hbm, hbm],
        out_specs=vmem,
        scratch_shapes=[pltpu.VMEM((2 * TX, LINES, SIDE), BF)] * (PARTS * TZ)
        + [pltpu.VMEM((PARTS, TOP + 1, COUNT, LINES, SIDE), BF)] * 2
        + [
            pltpu.SMEM((1, COUNT), jnp.int32),
            pltpu.SMEM((1, COUNT), jnp.int32),
            pltpu.SMEM((1, COUNT), jnp.int32),
            pltpu.SMEM((1, ANGLES), jnp.int32),
            pltpu.SMEM((ANGLES,), F32),
            pltpu.VMEM((COUNT, 2, SIDE, SIDE), BF),
            pltpu.VMEM((2, SIDE, SIDE), F32),
            pltpu.VMEM((2 * SIDE, 2 * SIDE), BF),
            pltpu.VMEM((2 * SIDE, 2 * SIDE), BF),
            pltpu.VMEM((1, 3, 3, CH), BF),
            pltpu.VMEM((1, 3, 3, CH), BF),
            pltpu.VMEM((8, 128), jnp.int32),
            pltpu.VMEM((TZ, 8, 128), jnp.int32),
            pltpu.VMEM((2 * SIDE, COUNT * SIDE), F32),
            pltpu.VMEM((H, COUNT * SIDE), BF),
            pltpu.VMEM((COUNT * SIDE, W), BF),
            pltpu.VMEM((CHUNKS, TX, rows_x, WIDE), BF),
            pltpu.VMEM((CHUNKS, TX, rows_x, WIDE), BF),
            pltpu.VMEM((CHUNKS, TZ, STRIP, WIDE), BF),
            pltpu.VMEM((CHUNKS, TZ, STRIP, WIDE), BF),
            pltpu.VMEM((TZ, TX, STRIP, LAST), BF),
            pltpu.VMEM((TZ, TX, STRIP, LAST), BF),
            pltpu.VMEM((TX, STRIP, LAST), BF),
            pltpu.VMEM((TX, STRIP, LAST), BF),
            pltpu.VMEM((ANGLES, 16, 128), BF),
            pltpu.VMEM((ANGLES, 16, 128), BF),
            pltpu.VMEM((ANGLES, 16, 128), BF),
            pltpu.VMEM((ANGLES * 16, 128), F32),
            pltpu.VMEM((SHIFTS * XW, 2 * ANGLES), BF),
            pltpu.VMEM((CH * XW, 128), BF),
            pltpu.VMEM((3 * XW, CH * XW), BF),
            dma((27,)),
            dma((16, TX)),
            dma((16, TX)),
            dma((2, PARTS, TOP + 1)),
            dma((2, PARTS, TOP + 1)),
            dma((TZ,)),
            dma((TZ,)),
            dma((CHUNKS, TX)),
            dma((CHUNKS, TX)),
            dma((CHUNKS, TZ)),
            dma((CHUNKS, TZ)),
            dma((TZ,)),
            dma((TZ,)),
            dma((TX,)),
            dma((TX,)),
            dma((ANGLES,)),
            dma((ANGLES,)),
        ],
        compiler_params=pltpu.CompilerParams(
            collective_id=0, has_side_effects=True, vmem_limit_bytes=32 * 1024 * 1024
        ),
        name="frames_to_volume",
    )(
        stay(owners.reshape(1, COUNT)), stay(scan_rows), stay(scan_cols), stay(slab_rows), stay(angle_tan), stay(patches[0]), stay(magnitudes[0]),
        stay(probe), stay(table), stay(table_t), stay(prior_in.transpose(1, 2, 3, 0)),
        stay(prior_out.transpose(0, 2, 3, 1)),
    )
    return volume[None]


def solution(mesh):
    placed = (
        P("angle", "tile", None, None, None),
        P("angle", "tile", None, None),
        P(),
        P("angle", "tile", None),
        P("angle", "tile"),
        P("angle", "tile"),
        P("tile", None),
        P(),
        P(),
        P(),
    )
    return jax.shard_map(
        body, mesh=mesh, in_specs=placed, out_specs=P("tile", "angle", None, None), check_vma=False
    )
```
